1024 devices in a mesh: expert: 32 (over z, core), dp: 32 (over x, y).
Axes of the slice: x: 4, y: 8, z: 16, core: 2. Of those that a mesh axis runs over, the one named last changes fastest.
Arguments:
- tokens: bfloat16 [1024, 4096], P('expert', 'dp'), may hold values from -6 to 6
- grad_out: bfloat16 [1024, 4096], P('expert', 'dp'), may hold values from -3 to 3
- expert_ids: int32 [1024, 8], P('expert'), may hold values from 0 to 31, all different within a row; in each aligned block of 32 rows (0 to 31, 32 to 63, ...) at most 16 rows name the same one
- probs: bfloat16 [1024, 8], P('expert'), may hold values from 0.099609375 to 0.5
- gate_weight: bfloat16 [32, 4096, 1536], P('expert', 'dp'), may hold values from -0.09375 to 0.09375
- up_weight: bfloat16 [32, 4096, 1536], P('expert', 'dp'), may hold values from -0.09375 to 0.09375
- down_weight: bfloat16 [32, 1536, 4096], P('expert', None, 'dp'), may hold values from -0.15625 to 0.15625
Outputs:
- grad_tokens: bfloat16 [1024, 4096], P('expert', 'dp')
- grad_probs: bfloat16 [1024, 8], P('expert')
- grad_gate: float32 [32, 4096, 1536], P('expert', 'dp')
- grad_up: float32 [32, 4096, 1536], P('expert', 'dp')
- grad_down: float32 [32, 1536, 4096], P('expert', None, 'dp')
The draws below stay inside these ranges and needn't reach their ends.
Inputs may be any that keep to these rules, and one draw needn't show every extreme that they name: `expert_ids`: each row names 8 different experts. Among the routes of the 32 tokens of one index of expert no expert is named more than 16 times, and in at least one such block some expert is named exactly 16 times.
All inputs are finite; a program needn't handle non-finite values.
Results may differ from the reference program's by a relative error of at most 0.0057.
Values may be sent and summed in bfloat16 or wider, within the bound.
A program may use at most 64 MiB of HBM per device.

```python
import math
import jax
import jax.numpy as jnp
import numpy as np
from jax import lax

D = 4096
FF = 1536
TOP = 8
TOK_DEV = 32
EXPERTS = 32
TOKENS = 1024
CAP = 16
ROWS = 512


def block_scale(stream_key, shape, split, least, top_value):
    def one(axis_at, blocks):
        heights = jax.random.uniform(jax.random.fold_in(jax.random.fold_in(stream_key, 6), axis_at), (blocks,), jnp.float32, least / len(split), top_value / len(split))
        return jnp.repeat(jnp.exp(heights), shape[axis_at] // blocks).reshape((-1,) + (1,) * (len(shape) - axis_at - 1))

    loudness = one(*split[0])
    for cut in split[1:]:
        loudness = loudness * one(*cut)
    return loudness


def assign_block(key, own, number, rows, count, top, bound, lean):
    order = jax.random.permutation(key, count)
    packed, common = portions_of(count, rows * top, bound, lean, True), portions_of(count, rows * top, bound, lean, False)
    places = jnp.arange(count)

    def named(sizes, turn):
        used = int((sizes > 0).sum())
        fixed = max(1, used // 4)
        moved = fixed + (places - fixed + turn * (used - fixed)) % max(1, count - fixed)
        return jnp.zeros((count,), jnp.int32).at[order[jnp.where(places < fixed, places, moved)]].set(jnp.asarray(sizes, jnp.int32))

    sizes = jnp.where(number % 4 == 0, named(packed, number // 4), named(common, number - number // 4 - 1))
    mixed = jax.random.permutation(jax.random.fold_in(own, 3), count)
    source_of, receiver = mixed[0:count // 2 * 2:2], mixed[1:count // 2 * 2:2]
    margin = jnp.minimum(sizes[source_of] - 1, bound - sizes[receiver]) // 2
    margin = jnp.where((source_of == order[0]) | (receiver == order[0]) | (sizes[receiver] == 0), 0, jnp.maximum(margin, 0))
    moved = jax.random.randint(jax.random.fold_in(own, 4), (count // 2,), 0, 1 << 20) % (margin + 1)
    sizes = sizes.at[source_of].add(-moved).at[receiver].add(moved)
    members = jnp.searchsorted(jnp.cumsum(sizes), jnp.arange(rows * top), side="right").astype(jnp.int32)
    table = members.reshape(top, rows).T
    table = table[jax.random.permutation(jax.random.fold_in(own, 1), rows)]
    turn = jax.random.randint(jax.random.fold_in(own, 2), (rows, 1), 0, top)
    return jnp.take_along_axis(table, (jnp.arange(top)[None, :] + turn) % top, axis=1)


def portions_of(count, total, limit, skew, full):
    portions = [(1 << 20) // math.isqrt(rank ** skew) + 1 for rank in range(1, count + 1)]
    largest = limit if full else min(limit, max(-(-total // count), total * portions[0] // sum(portions)))
    least = 1 if total - largest >= count - 1 else 0
    given, surplus = [largest] + [least] * (count - 1), total - largest - least * (count - 1)
    while surplus > 0:
        movable = [i for i in range(1, count) if given[i] < largest] or [i for i in range(1, count) if given[i] < limit]
        whole, left = sum([portions[i] for i in movable]), surplus
        for i in movable:
            addition = min(limit - given[i], max(1, left * portions[i] // whole), surplus)
            given[i] = given[i] + addition
            surplus = surplus - addition
    return np.array(given)


def normal_values(key, extent, width, most, shards=(), kind=jnp.bfloat16):
    entries = width * jax.random.normal(key, extent, jnp.float32)
    if shards:
        entries = entries * block_scale(key, extent, shards, -0.22, 0.18)
    return jnp.clip(entries, -most, most).astype(kind)


def setup_inputs(seed: int = 0) -> dict:
    key_list = jax.random.split(jax.random.key(seed), 8)
    tokens = normal_values(key_list[0], (TOKENS, D), 1.0, 6.0, ((0, 32), (1, 32)))
    grad_out = normal_values(key_list[1], (TOKENS, D), 0.5, 3.0, ((0, 32), (1, 32)))
    expert_ids_keys = jax.random.split(jax.random.fold_in(key_list[2], 1), TOKENS // TOK_DEV)
    expert_ids_turns = jax.random.permutation(jax.random.fold_in(key_list[2], 3), TOKENS // TOK_DEV)
    expert_ids = jax.vmap(lambda own, number: assign_block(jax.random.fold_in(key_list[2], 2), own, number, TOK_DEV, EXPERTS, TOP, CAP, 1))(expert_ids_keys, expert_ids_turns).reshape((TOKENS, TOP))
    probs = jnp.clip(0.099609375 + 0.40039062 * jax.random.uniform(key_list[3], (TOKENS, TOP), jnp.float32) ** block_scale(key_list[3], (TOKENS, TOP), ((0, 32),), -0.2, 0.2), 0.099609375, 0.5).astype(jnp.bfloat16)
    gate_weight = normal_values(key_list[4], (EXPERTS, D, FF), D ** -0.5, 0.09375, ((0, 32), (1, 32)))
    up_weight = normal_values(key_list[5], (EXPERTS, D, FF), D ** -0.5, 0.09375, ((0, 32), (1, 32)))
    down_weight = normal_values(key_list[6], (EXPERTS, FF, D), FF ** -0.5, 0.15625, ((0, 32), (2, 32)))
    return {"tokens": tokens, "grad_out": grad_out, "expert_ids": expert_ids, "probs": probs, "gate_weight": gate_weight, "up_weight": up_weight, "down_weight": down_weight}


def swiglu_backward(gate_sum, up_sum, back_sum, route_weight):
    sigmoid_gate = jax.nn.sigmoid(gate_sum)
    active = gate_sum * sigmoid_gate
    product = active * up_sum
    grad_weight = jnp.sum(back_sum * product, axis=1).astype(jnp.bfloat16)
    scaled = route_weight[:, None] * back_sum
    grad_gate_pre = (scaled * up_sum * sigmoid_gate * (1.0 + gate_sum * (1.0 - sigmoid_gate))).astype(jnp.bfloat16)
    grad_up_pre = (scaled * active).astype(jnp.bfloat16)
    weighted = (route_weight[:, None] * product).astype(jnp.bfloat16)
    return jnp.concatenate((weighted, grad_gate_pre, grad_up_pre), axis=1), grad_weight


def reference(tokens, grad_out, expert_ids, probs, gate_weight, up_weight, down_weight):
    routes = TOKENS * TOP
    flat_ids = expert_ids.reshape(routes).astype(jnp.int32)
    onehot = (flat_ids[:, None] == jnp.arange(EXPERTS, dtype=jnp.int32)[None, :]).astype(jnp.int32)
    rank_of = jnp.sum((jnp.cumsum(onehot, axis=0) - onehot) * onehot, axis=1).astype(jnp.int32)
    slot_table = jnp.full((EXPERTS, ROWS), routes, jnp.int32).at[flat_ids, rank_of].set(jnp.arange(routes, dtype=jnp.int32))
    spread_x = jnp.concatenate((jnp.repeat(tokens.astype(jnp.float32), TOP, axis=0), jnp.zeros((1, D), jnp.float32)), axis=0)
    spread_dy = jnp.concatenate((jnp.repeat(grad_out.astype(jnp.float32), TOP, axis=0), jnp.zeros((1, D), jnp.float32)), axis=0)
    spread_p = jnp.concatenate((probs.reshape(routes).astype(jnp.float32), jnp.zeros((1,), jnp.float32)))

    def one_expert(operands):
        row_index, w_gate, w_up, w_down = operands
        gate_full = w_gate.astype(jnp.float32)
        up_full = w_up.astype(jnp.float32)
        down_full = w_down.astype(jnp.float32)
        rows_x = spread_x[row_index]
        rows_dy = spread_dy[row_index]
        rows_p = spread_p[row_index]
        gate_sum = jnp.dot(rows_x, gate_full, preferred_element_type=jnp.float32)
        up_sum = jnp.dot(rows_x, up_full, preferred_element_type=jnp.float32)
        back_sum = jnp.dot(rows_dy, down_full.T, preferred_element_type=jnp.float32)
        stacked, grad_weight = swiglu_backward(gate_sum, up_sum, back_sum, rows_p)
        weighted = stacked[:, :FF].astype(jnp.float32)
        grad_gate_pre = stacked[:, FF:2 * FF].astype(jnp.float32)
        grad_up_pre = stacked[:, 2 * FF:].astype(jnp.float32)
        grad_gate = jnp.dot(rows_x.T, grad_gate_pre, preferred_element_type=jnp.float32)
        grad_up = jnp.dot(rows_x.T, grad_up_pre, preferred_element_type=jnp.float32)
        grad_down = jnp.dot(weighted.T, rows_dy, preferred_element_type=jnp.float32)
        route_dx = (jnp.dot(grad_gate_pre, gate_full.T, preferred_element_type=jnp.float32)
                    + jnp.dot(grad_up_pre, up_full.T, preferred_element_type=jnp.float32)).astype(jnp.bfloat16)
        return grad_gate, grad_up, grad_down, route_dx, grad_weight

    grad_gate, grad_up, grad_down, route_dx, grad_weight = lax.map(one_expert, (slot_table, gate_weight, up_weight, down_weight))
    every_dx = jnp.zeros((routes + 1, D), jnp.bfloat16).at[slot_table.reshape(-1)].set(route_dx.reshape(EXPERTS * ROWS, D))
    every_dp = jnp.zeros((routes + 1,), jnp.bfloat16).at[slot_table.reshape(-1)].set(grad_weight.reshape(EXPERTS * ROWS))
    grad_tokens = jnp.sum(every_dx[:routes].astype(jnp.float32).reshape(TOKENS, TOP, D), axis=1).astype(jnp.bfloat16)
    grad_probs = every_dp[:routes].reshape(TOKENS, TOP)
    return grad_tokens, grad_probs, grad_gate, grad_up, grad_down
```

```python
import functools

import jax
import jax.numpy as jnp
from jax import lax
from jax.experimental import pallas as pl
from jax.experimental.pallas import tpu as pltpu
from jax.sharding import PartitionSpec as P

MESH = pl.DeviceIdType.MESH
F32, BF16 = jnp.float32, jnp.bfloat16
RING_X = 4
RS_SPLIT = (1024, 512)
AG_SPLIT = (896, 640)


def nt(a, b):
    return lax.dot_general(a, b, (((1,), (1,)), ((), ())), preferred_element_type=F32)


def nn(a, b):
    return jnp.dot(a, b, preferred_element_type=F32)


def iota(shape, dim):
    return lax.broadcasted_iota(jnp.int32, shape, dim)


def pieces(width, step=256):
    return [(c, min(step, width - c)) for c in range(0, width, step)]


class Ring:
    def __init__(self, at, size, turn):
        self.at, self.size, self.turn = at, size, turn
        half = size // 2
        self.reach = {"f": half, "n": size - 1 - half}
        self.away = [("f", t) for t in range(1, half + 1)]
        self.away += [("n", t) for t in range(1, size - half)]

    def shift(self, hops):
        return lax.rem(self.at + self.turn * hops + 2 * self.size, self.size)

    def target(self, offset):
        if offset is None:
            return self.at
        side, t = offset
        return self.shift(-t if side == "f" else t)

    def origin(self, offset):
        if offset is None:
            return self.at
        side, t = offset
        return self.shift(t if side == "f" else -t)

    def following(self, side):
        return self.shift(-1 if side == "f" else 1)


def dist(offset):
    return 0 if offset is None else offset[1]


def kernel(ring_x, ring_y, cap, rs_split, ag_split, tokens, grad_out, ids, probs, w_gate, w_up, w_down,
           o_tokens, o_probs, o_gate, o_up, o_down,
           hot, hot_t, send_rows, rows, x_t, dy_t, prob_send, prob_recv, partial,
           a1_send, a1_recv, a2_send, a2_recv, b1_send, b1_recv, b2_send, b2_recv,
           gathered, dx_send, back, dp_send, dp_recv, spread,
           disp_s, disp_r, prob_s, prob_r, a1_s, a1_r, a2_s, a2_r, b1_s, b1_r, b2_s, b2_r,
           ga_s, ga_r, gb_s, gb_r, ret_s, ret_r, dp_s, dp_r, bc_s, bc_r):
    me, mine = lax.axis_index("expert"), lax.axis_index("dp")
    experts, group = lax.axis_size("expert"), ring_x * ring_y
    tok, features = tokens.shape
    top, hidden = ids.shape[1], w_gate.shape[1]
    slots = experts * cap
    turn = 1 - 2 * lax.rem(me, 2)
    rx = Ring(mine // ring_y, ring_x, turn)
    ry = Ring(lax.rem(mine, ring_y), ring_y, turn)
    ring_a, ring_b = (rx, ry), (ry, rx)

    def block_at(first, second, rings):
        bx, by = (first, second) if rings[0] is rx else (second, first)
        return bx * ring_y + by

    def neighbour(ring, side):
        to = ring.following(side)
        return {"dp": to * ring_y + ry.at} if ring is rx else {"dp": rx.at * ring_y + to}

    barrier = pltpu.get_barrier_semaphore()

    def greet(where):
        pl.semaphore_signal(barrier, inc=1, device_id=where, device_id_type=MESH)

    for r in range(1, experts):
        greet({"expert": lax.rem(me + r, experts)})
    greeted = experts - 1
    for ring in (rx, ry):
        for side in ("f", "n"):
            if ring.reach[side]:
                greet(neighbour(ring, side))
                greeted += 1
    on_diagonal = me == mine

    @pl.when(jnp.logical_not(on_diagonal))
    def _():
        greet({"dp": me})

    ids_b = ids[...].astype(F32).astype(BF16)
    eye = (iota((top, top), 0) == iota((top, top), 1)).astype(F32).astype(BF16)
    ids_t = nt(eye, ids_b)
    probs_t = nt(eye, probs[...])
    expert_row = iota((experts, tok), 0).astype(F32)
    chosen = jnp.zeros((experts, tok), F32)
    weight = jnp.zeros((experts, tok), F32)
    for k in range(top):
        hit = ids_t[k:k + 1, :] == expert_row
        chosen = chosen + jnp.where(hit, 1.0, 0.0)
        weight = weight + jnp.where(hit, probs_t[k:k + 1, :], 0.0)
    earlier = jnp.where(iota((tok, tok), 0) < iota((tok, tok), 1), 1.0, 0.0).astype(BF16)
    rank = jnp.where(chosen > 0.5, nn(chosen.astype(BF16), earlier), 128.0).astype(BF16)
    owner = jnp.where(iota((slots, experts), 0) // cap == iota((slots, experts), 1), 1.0, 0.0).astype(BF16)
    owner_t = jnp.where(iota((experts, slots), 1) // cap == iota((experts, slots), 0), 1.0, 0.0).astype(BF16)
    slot_col = lax.rem(iota((slots, tok), 0), cap).astype(F32)
    slot_row = lax.rem(iota((tok, slots), 1), cap).astype(F32)
    one_hot = jnp.where(nn(owner, rank) == slot_col, 1.0, 0.0)
    hot[...] = one_hot.astype(BF16)
    eye_t = jnp.where(iota((tok, tok), 0) == iota((tok, tok), 1), 1.0, 0.0).astype(BF16)
    rank_t = nt(eye_t, rank)
    hot_t[...] = jnp.where(nn(rank_t.astype(BF16), owner_t) == slot_row, 1.0, 0.0).astype(BF16)
    send_rows[:, :, 0:features] = nn(hot[...], tokens[...]).astype(BF16).reshape(experts, cap, features)
    send_rows[:, :, features:2 * features] = nn(hot[...], grad_out[...]).astype(BF16).reshape(experts, cap, features)
    slot_weight = jnp.sum(one_hot * nn(owner, weight.astype(BF16)), axis=1, keepdims=True)
    lane_slot = iota((slots, 128), 1) == lax.rem(iota((slots, 128), 0), cap)
    weight_rows = nn(owner_t, jnp.where(lane_slot, slot_weight, 0.0).astype(BF16))
    for e in range(experts):
        prob_send[e] = weight_rows[e:e + 1, :]
    rows[me] = send_rows[me]

    @pl.when(on_diagonal)
    def _():
        prob_recv[...] = prob_send[me]
        pl.semaphore_wait(barrier, greeted + group - 1)

    @pl.when(jnp.logical_not(on_diagonal))
    def _():
        pl.semaphore_wait(barrier, greeted)

    dispatch = []
    for r in range(1, experts):
        to = lax.rem(me + r, experts)
        copy = pltpu.make_async_remote_copy(
            send_rows.at[to], rows.at[me], disp_s.at[r], disp_r.at[r], {"expert": to}, MESH)
        copy.start()
        dispatch.append(copy)

    def prob_copy(r):
        to = lax.rem(me + r, experts)
        return pltpu.make_async_remote_copy(
            prob_send.at[to], prob_recv, prob_s.at[r], prob_r, {"expert": to}, MESH)

    @pl.when(on_diagonal)
    def _():
        for r in range(1, experts):
            prob_copy(r).start()

    for r in range(1, experts):
        dispatch[r - 1].wait_recv()

    rs_a, rs_b = rs_split
    width_a, width_b = 3 * rs_a, 3 * rs_b
    half = group // 2
    for part in range(2):
        blk = slice(part * half, (part + 1) * half)
        x = rows[blk, :, 0:features].reshape(half * cap, features)
        dy = rows[blk, :, features:2 * features].reshape(half * cap, features)
        for at, width, base in ((0, rs_a, 0), (rs_a, rs_b, width_a)):
            for c, n in pieces(width):
                for j, value in enumerate((
                    nn(x, w_gate[:, at + c:at + c + n]),
                    nn(x, w_up[:, at + c:at + c + n]),
                    nt(dy, w_down[at + c:at + c + n, :]),
                )):
                    col = base + j * width + c
                    partial[blk, :, col:col + n] = value.reshape(half, cap, n)

    plans = []
    for rings, base, width, bufs in (
        (ring_a, 0, width_a, (a1_send, a1_recv, a1_s, a1_r, a2_send, a2_recv, a2_s, a2_r)),
        (ring_b, width_a, width_b, (b1_send, b1_recv, b1_s, b1_r, b2_send, b2_recv, b2_s, b2_r)),
    ):
        first, second = rings
        inner = [None] + second.away
        one = {(o1, o2): i for i, (o1, o2) in enumerate((o1, o2) for o1 in first.away for o2 in inner)}
        two = {o2: i for i, o2 in enumerate(second.away)}
        plans.append((rings, base, width, bufs, one, two))

    def one_copy(plan, key):
        rings, _, _, bufs, one, _ = plan
        i = one[key]
        return pltpu.make_async_remote_copy(
            bufs[0].at[i], bufs[1].at[i], bufs[2].at[i], bufs[3].at[i], neighbour(rings[0], key[0][0]), MESH)

    def two_copy(plan, key):
        rings, _, _, bufs, _, two = plan
        i = two[key]
        return pltpu.make_async_remote_copy(
            bufs[4].at[i], bufs[5].at[i], bufs[6].at[i], bufs[7].at[i], neighbour(rings[1], key[0]), MESH)

    def arrived_one(plan, key, total):
        one_copy(plan, key).wait_recv()
        return total + plan[3][1][plan[4][key]].astype(F32)

    def arrived_two(plan, key, total):
        two_copy(plan, key).wait_recv()
        return total + plan[3][5][plan[5][key]]

    def own(plan, o1, o2):
        rings, base, width = plan[:3]
        return partial[block_at(rings[0].target(o1), rings[1].target(o2), rings), :, base:base + width]

    def reduced_first(plan, o2):
        total = own(plan, None, o2)
        for side in ("f", "n"):
            if plan[0][0].reach[side]:
                total = arrived_one(plan, ((side, 1), o2), total)
        return total

    furthest = ring_x // 2 + ring_y // 2
    for steps in range(furthest, 0, -1):
        for plan in plans:
            first, second = plan[0]
            for o1 in [None] + first.away:
                for o2 in [None] + second.away:
                    if dist(o1) + dist(o2) != steps:
                        continue
                    if o1 is not None:
                        side, t = o1
                        total = own(plan, o1, o2)
                        if t < first.reach[side]:
                            total = arrived_one(plan, ((side, t + 1), o2), total)
                        plan[3][0][plan[4][(o1, o2)]] = total.astype(BF16)
                        one_copy(plan, (o1, o2)).start()
                    else:
                        side, t = o2
                        total = reduced_first(plan, o2)
                        if t < second.reach[side]:
                            total = arrived_two(plan, (side, t + 1), total)
                        plan[3][4][plan[5][o2]] = total
                        two_copy(plan, o2).start()
    done = []
    for plan in plans:
        total = reduced_first(plan, None)
        for side in ("f", "n"):
            if plan[0][1].reach[side]:
                total = arrived_two(plan, (side, 1), total)
        done.append(total)

    @pl.when(jnp.logical_not(on_diagonal))
    def _():
        prob_copy(1).wait_recv()

    diagonal = iota((cap, 128), 0) == iota((cap, 128), 1)
    weight_col = jnp.sum(jnp.where(diagonal, prob_recv[...], 0.0), axis=1, keepdims=True)
    ag_a, ag_b = ag_split
    full_a = 3 * ag_a
    grad_weight = jnp.zeros((cap, 1), F32)
    for total, at, width in ((done[0], 0, rs_a), (done[1], rs_a, rs_b)):
        gate, up, bk = (total[:, j * width:(j + 1) * width] for j in range(3))
        sig = jax.nn.sigmoid(gate)
        active = gate * sig
        product = active * up
        grad_weight = grad_weight + jnp.sum(bk * product, axis=1, keepdims=True)
        scaled = weight_col * bk
        results = (
            (weight_col * product).astype(BF16),
            (scaled * up * sig * (1.0 + gate * (1.0 - sig))).astype(BF16),
            (scaled * active).astype(BF16),
        )
        for j, value in enumerate(results):
            for lo, hi, start, n in ((0, ag_a, 0, ag_a), (ag_a, ag_a + ag_b, full_a, ag_b)):
                a, b = max(lo, at), min(hi, at + width)
                if a < b:
                    col = start + j * n + a - lo
                    gathered[mine, :, col:col + b - a] = value[:, a - at:b - at]

    gathers = []
    for rings, base, width, sems in (
        (ring_b, 0, full_a, (ga_s, ga_r)), (ring_a, full_a, 3 * ag_b, (gb_s, gb_r))):
        first, second = rings
        keys = [("1", o1) for o1 in first.away]
        keys += [("2", o1, o2) for o1 in [None] + first.away for o2 in second.away]
        gathers.append((rings, base, width, sems, {k: i for i, k in enumerate(keys)}))

    def gather_copy(plan, key):
        rings, base, width, sems, index = plan
        if key[0] == "1":
            side, t = key[1]
            before = (side, t - 1) if t > 1 else None
            blk = block_at(rings[0].origin(before), rings[1].at, rings)
            to = neighbour(rings[0], side)
        else:
            side, t = key[2]
            before = (side, t - 1) if t > 1 else None
            blk = block_at(rings[0].origin(key[1]), rings[1].origin(before), rings)
            to = neighbour(rings[1], side)
        ref = gathered.at[blk, :, base:base + width]
        i = index[key]
        return pltpu.make_async_remote_copy(ref, ref, sems[0].at[i], sems[1].at[i], to, MESH)

    def gather_wait(plan, key):
        rings, base, width, sems, index = plan
        if key[0] == "1":
            blk = block_at(rings[0].origin(key[1]), rings[1].at, rings)
            to = neighbour(rings[0], key[1][0])
        else:
            blk = block_at(rings[0].origin(key[1]), rings[1].origin(key[2]), rings)
            to = neighbour(rings[1], key[2][0])
        ref = gathered.at[blk, :, base:base + width]
        i = index[key]
        pltpu.make_async_remote_copy(ref, ref, sems[0].at[i], sems[1].at[i], to, MESH).wait_recv()

    def onward(plan, o1):
        for side in ("f", "n"):
            if plan[0][1].reach[side]:
                gather_copy(plan, ("2", o1, (side, 1))).start()

    def gather_step(steps):
        for plan in gathers:
            first, second = plan[0]
            for o1 in [None] + first.away:
                for o2 in [None] + second.away:
                    if dist(o1) + dist(o2) != steps:
                        continue
                    if o2 is None:
                        side, t = o1
                        gather_wait(plan, ("1", o1))
                        if t < first.reach[side]:
                            gather_copy(plan, ("1", (side, t + 1))).start()
                        onward(plan, o1)
                    else:
                        side, t = o2
                        gather_wait(plan, ("2", o1, o2))
                        if t < second.reach[side]:
                            gather_copy(plan, ("2", o1, (side, t + 1))).start()

    for plan in gathers:
        for side in ("f", "n"):
            if plan[0][0].reach[side]:
                gather_copy(plan, ("1", (side, 1))).start()
        onward(plan, None)

    rounded = grad_weight.astype(BF16).astype(F32)
    dp_send[...] = jnp.sum(jnp.where(diagonal, rounded, 0.0), axis=0, keepdims=True)

    def dp_copy(slot, where):
        return pltpu.make_async_remote_copy(
            dp_send, dp_recv.at[slot], dp_s, dp_r.at[slot], {"expert": where}, MESH)

    @pl.when(jnp.logical_not(on_diagonal))
    def _():
        dp_copy(me, mine).start()

    for r in range(1, experts):
        dispatch[r - 1].wait_send()
    for rows_of in range(group // 8):
        x = rows[rows_of * 8:rows_of * 8 + 8]
        x_t[:, rows_of * 8 * cap:(rows_of + 1) * 8 * cap] = (
            x[:, :, 0:features].reshape(8 * cap, features).astype(F32).T.astype(BF16))
        dy_t[:, rows_of * 8 * cap:(rows_of + 1) * 8 * cap] = (
            x[:, :, features:2 * features].reshape(8 * cap, features).astype(F32).T.astype(BF16))
    gather_step(1)
    gather_step(2)

    def spread_copy(r):
        return pltpu.make_async_remote_copy(
            spread, spread, bc_s.at[r], bc_r, {"dp": lax.rem(me + r, group)}, MESH)

    @pl.when(on_diagonal)
    def _():
        for r in range(1, experts):
            prob_copy(r).wait_send()
            dp_copy(lax.rem(me + r, experts), lax.rem(me + r, experts)).wait_recv()
        dp_recv[me] = dp_send[...]
        values = dp_recv[...].reshape(experts, 128).astype(BF16)
        lane = iota((tok, 128), 1)
        result = jnp.zeros((tok, 128), F32)
        for k in range(top):
            pick = jnp.where(ids[:, k:k + 1] == iota((tok, experts), 1), 1.0, 0.0)
            row = nn(pick.astype(BF16), values)
            place = jnp.sum(jnp.where(pick > 0.5, rank_t, 0.0), axis=1, keepdims=True)
            found = jnp.sum(jnp.where(lane.astype(F32) == place, row, 0.0), axis=1, keepdims=True)
            result = jnp.where(lane == k, found, result)
        spread[...] = result.astype(BF16)
        for r in range(1, group):
            spread_copy(r).start()

    for steps in range(3, furthest + 1):
        gather_step(steps)

    def piece(blk, j, part):
        at, n = ((0, ag_a), (full_a, ag_b))[part]
        return gathered[blk, :, at + j * n:at + (j + 1) * n]

    for first in range(0, group, 8):
        blk = slice(first, first + 8)
        total = jnp.zeros((8 * cap, features), F32)
        for part, (at, n) in enumerate(((0, ag_a), (ag_a, ag_b))):
            total = total + nt(piece(blk, 1, part).reshape(8 * cap, n), w_gate[:, at:at + n])
            total = total + nt(piece(blk, 2, part).reshape(8 * cap, n), w_up[:, at:at + n])
        dx_send[blk] = total.astype(BF16).reshape(8, cap, features)
    returns = []
    for r in range(1, experts):
        to = lax.rem(me + r, experts)
        copy = pltpu.make_async_remote_copy(
            dx_send.at[to], back.at[me], ret_s.at[r], ret_r.at[r], {"expert": to}, MESH)
        copy.start()
        returns.append(copy)
    back[me] = dx_send[me]

    for part, (at, n) in enumerate(((0, ag_a), (ag_a, ag_b))):
        for c, m in pieces(n):
            start = (0, full_a)[part] + c
            for j, (left, out) in enumerate(((dy_t, o_down), (x_t, o_gate), (x_t, o_up))):
                right = gathered[:, :, start + j * n:start + j * n + m].reshape(slots, m)
                value = nn(left[...], right)
                if j == 0:
                    out[at + c:at + c + m, :] = value.T
                else:
                    out[:, at + c:at + c + m] = value

    @pl.when(jnp.logical_not(on_diagonal))
    def _():
        spread_copy(1).wait_recv()
        dp_copy(me, mine).wait_send()

    @pl.when(on_diagonal)
    def _():
        for r in range(1, group):
            spread_copy(r).wait_send()

    o_probs[...] = spread[:, 0:top]
    for plan in plans:
        for key in plan[4]:
            one_copy(plan, key).wait_send()
        for key in plan[5]:
            two_copy(plan, key).wait_send()
    for plan in gathers:
        for key in plan[4]:
            gather_copy(plan, key).wait_send()
    for copy in returns:
        copy.wait_recv()
    o_tokens[...] = nn(hot_t[...], back[...].reshape(slots, features)).astype(BF16)
    for copy in returns:
        copy.wait_send()


def per_device(tokens, grad_out, expert_ids, probs, gate_weight, up_weight, down_weight):
    tok, features = tokens.shape
    top = expert_ids.shape[1]
    hidden = gate_weight.shape[2]
    experts, group = lax.axis_size("expert"), lax.axis_size("dp")
    cap = min(tok, 2 * tok * top // experts)
    ring_x, ring_y = RING_X, group // RING_X
    slots = experts * cap
    wide_a, wide_b = 3 * RS_SPLIT[0], 3 * RS_SPLIT[1]
    n_a1, n_a2 = (ring_x - 1) * ring_y, ring_y - 1
    n_b1, n_b2 = (ring_y - 1) * ring_x, ring_x - 1
    vmem = pltpu.VMEM
    dma = pltpu.SemaphoreType.DMA
    buffers = [
        vmem((slots, tok), BF16), vmem((tok, slots), BF16),
        vmem((experts, cap, 2 * features), BF16), vmem((experts, cap, 2 * features), BF16),
        vmem((features, slots), BF16), vmem((features, slots), BF16),
        vmem((experts, 1, 128), F32), vmem((1, 128), F32),
        vmem((group, cap, 3 * hidden), F32),
        vmem((n_a1, cap, wide_a), BF16), vmem((n_a1, cap, wide_a), BF16),
        vmem((n_a2, cap, wide_a), F32), vmem((n_a2, cap, wide_a), F32),
        vmem((n_b1, cap, wide_b), BF16), vmem((n_b1, cap, wide_b), BF16),
        vmem((n_b2, cap, wide_b), F32), vmem((n_b2, cap, wide_b), F32),
        vmem((group, cap, 3 * hidden), BF16),
        vmem((experts, cap, features), BF16), vmem((experts, cap, features), BF16),
        vmem((1, 128), F32), vmem((experts, 1, 128), F32), vmem((tok, 128), BF16),
    ]
    sems = [
        dma((experts,)), dma((experts,)), dma((experts,)), dma(()),
        dma((n_a1,)), dma((n_a1,)), dma((n_a2,)), dma((n_a2,)),
        dma((n_b1,)), dma((n_b1,)), dma((n_b2,)), dma((n_b2,)),
        dma((n_b2 * ring_y + n_a2,)), dma((n_b2 * ring_y + n_a2,)),
        dma((n_a2 * ring_x + n_b2,)), dma((n_a2 * ring_x + n_b2,)),
        dma((experts,)), dma((experts,)), dma(()), dma((experts,)), dma((group,)), dma(()),
    ]
    flops = 2 * slots * features * hidden * 8
    out = pl.pallas_call(
        functools.partial(kernel, ring_x, ring_y, cap, RS_SPLIT, AG_SPLIT),
        out_shape=(
            jax.ShapeDtypeStruct((tok, features), BF16),
            jax.ShapeDtypeStruct((tok, top), BF16),
            jax.ShapeDtypeStruct((features, hidden), F32),
            jax.ShapeDtypeStruct((features, hidden), F32),
            jax.ShapeDtypeStruct((hidden, features), F32),
        ),
        in_specs=[pl.BlockSpec(memory_space=pltpu.VMEM)] * 7,
        out_specs=[pl.BlockSpec(memory_space=pltpu.VMEM)] * 5,
        scratch_shapes=buffers + sems,
        compiler_params=pltpu.CompilerParams(
            collective_id=0, has_side_effects=True, vmem_limit_bytes=58 * 1024 * 1024),
        cost_estimate=pl.CostEstimate(flops=flops, bytes_accessed=4 * 1024 * 1024, transcendentals=0),
    )(tokens, grad_out, expert_ids, probs, gate_weight[0], up_weight[0], down_weight[0])
    grad_tokens, grad_probs, grad_gate, grad_up, grad_down = out
    return grad_tokens, grad_probs, grad_gate[None], grad_up[None], grad_down[None]


def solution(mesh):
    return jax.shard_map(
        per_device,
        mesh=mesh,
        in_specs=(
            P("expert", "dp"),
            P("expert", "dp"),
            P("expert", None),
            P("expert", None),
            P("expert", "dp", None),
            P("expert", "dp", None),
            P("expert", None, "dp"),
        ),
        out_specs=(
            P("expert", "dp"),
            P("expert", None),
            P("expert", "dp", None),
            P("expert", "dp", None),
            P("expert", None, "dp"),
        ),
        check_vma=False,
    )
```

```python
import functools

import jax
import jax.numpy as jnp
from jax import lax
from jax.experimental import pallas as pl
from jax.experimental.pallas import tpu as pltpu
from jax.sharding import PartitionSpec as P

MESH = pl.DeviceIdType.MESH
F32, BF16 = jnp.float32, jnp.bfloat16
RING_X = 4
RS_SPLIT = (1024, 512)
AG_SPLIT = (896, 640)
SENDS = (3, 4)
CUTS = 2


def nt(a, b):
    return lax.dot_general(a, b, (((1,), (1,)), ((), ())), preferred_element_type=F32)


def nn(a, b):
    return jnp.dot(a, b, preferred_element_type=F32)


def iota(shape, dim):
    return lax.broadcasted_iota(jnp.int32, shape, dim)


def pieces(width, step=256):
    return [(c, min(step, width - c)) for c in range(0, width, step)]


class Ring:
    def __init__(self, at, size, turn):
        self.at, self.size, self.turn = at, size, turn
        half = size // 2
        self.reach = {"f": half, "n": size - 1 - half}
        self.away = [("f", t) for t in range(1, half + 1)]
        self.away += [("n", t) for t in range(1, size - half)]

    def shift(self, hops):
        return lax.rem(self.at + self.turn * hops + 2 * self.size, self.size)

    def target(self, offset):
        if offset is None:
            return self.at
        side, t = offset
        return self.shift(-t if side == "f" else t)

    def origin(self, offset):
        if offset is None:
            return self.at
        side, t = offset
        return self.shift(t if side == "f" else -t)

    def following(self, side):
        return self.shift(-1 if side == "f" else 1)


def dist(offset):
    return 0 if offset is None else offset[1]


def kernel(ring_x, ring_y, cap, rs_split, ag_split, tokens, grad_out, ids, probs, h_gate, h_up, h_down,
           o_tokens, o_probs, o_gate, o_up, o_down,
           w_gate, w_up, w_down, g_gate, g_up, g_down,
           hot, hot_t, send_rows, rows, x_t, dy_t, prob_send, prob_recv, partial,
           a1_send, a1_recv, a2_send, a2_recv, b1_send, b1_recv, b2_send, b2_recv,
           gathered, dx_send, back, dp_send, dp_recv, spread,
           load_s, store_s, disp_s, disp_r, prob_s, prob_r, a1_s, a1_r, a2_s, a2_r, b1_s, b1_r, b2_s, b2_r,
           ga_s, ga_r, gb_s, gb_r, ret_s, ret_r, dp_s, dp_r, bc_s, bc_r):
    me, mine = lax.axis_index("expert"), lax.axis_index("dp")
    experts, group = lax.axis_size("expert"), ring_x * ring_y
    tok, features = tokens.shape
    top = ids.shape[0]
    slots = experts * cap
    turn = 1 - 2 * lax.rem(me, 2)
    rx = Ring(mine // ring_y, ring_x, turn)
    ry = Ring(lax.rem(mine, ring_y), ring_y, turn)
    ring_a, ring_b = (rx, ry), (ry, rx)

    def block_at(first, second, rings):
        bx, by = (first, second) if rings[0] is rx else (second, first)
        return bx * ring_y + by

    def neighbour(ring, side):
        to = ring.following(side)
        return {"dp": to * ring_y + ry.at} if ring is rx else {"dp": rx.at * ring_y + to}

    barrier = pltpu.get_barrier_semaphore()

    def greet(where):
        pl.semaphore_signal(barrier, inc=1, device_id=where, device_id_type=MESH)

    for r in range(1, experts):
        greet({"expert": lax.rem(me + r, experts)})
    greeted = experts - 1
    for ring in (rx, ry):
        for side in ("f", "n"):
            if ring.reach[side]:
                greet(neighbour(ring, side))
                greeted += 1
    on_diagonal = me == mine

    @pl.when(jnp.logical_not(on_diagonal))
    def _():
        greet({"dp": me})

    loads = [
        pltpu.make_async_copy(src, dst, load_s.at[i])
        for i, (src, dst) in enumerate(((h_gate, w_gate), (h_up, w_up), (h_down, w_down)))
    ]
    for copy in loads:
        copy.start()

    ids_t = ids[...].astype(F32)
    probs_t = probs[...].astype(F32)
    expert_row = iota((experts, tok), 0).astype(F32)
    chosen = jnp.zeros((experts, tok), F32)
    weight = jnp.zeros((experts, tok), F32)
    for k in range(top):
        hit = ids_t[k:k + 1, :] == expert_row
        chosen = chosen + jnp.where(hit, 1.0, 0.0)
        weight = weight + jnp.where(hit, probs_t[k:k + 1, :], 0.0)
    earlier = jnp.where(iota((tok, tok), 0) < iota((tok, tok), 1), 1.0, 0.0).astype(BF16)
    rank = jnp.where(chosen > 0.5, nn(chosen.astype(BF16), earlier), 128.0).astype(BF16)
    owner = jnp.where(iota((slots, experts), 0) // cap == iota((slots, experts), 1), 1.0, 0.0).astype(BF16)
    owner_t = jnp.where(iota((experts, slots), 1) // cap == iota((experts, slots), 0), 1.0, 0.0).astype(BF16)
    slot_col = lax.rem(iota((slots, tok), 0), cap).astype(F32)
    slot_row = lax.rem(iota((tok, slots), 1), cap).astype(F32)
    one_hot = jnp.where(nn(owner, rank) == slot_col, 1.0, 0.0)
    hot[...] = one_hot.astype(BF16)
    eye_t = jnp.where(iota((tok, tok), 0) == iota((tok, tok), 1), 1.0, 0.0).astype(BF16)
    rank_t = nt(eye_t, rank)
    hot_t[...] = jnp.where(nn(rank_t.astype(BF16), owner_t) == slot_row, 1.0, 0.0).astype(BF16)
    send_rows[:, :, 0:features] = nn(hot[...], tokens[...]).astype(BF16).reshape(experts, cap, features)
    send_rows[:, :, features:2 * features] = nn(hot[...], grad_out[...]).astype(BF16).reshape(experts, cap, features)
    slot_weight = jnp.sum(one_hot * nn(owner, weight.astype(BF16)), axis=1, keepdims=True)
    lane_slot = iota((slots, 128), 1) == lax.rem(iota((slots, 128), 0), cap)
    weight_rows = nn(owner_t, jnp.where(lane_slot, slot_weight, 0.0).astype(BF16))
    for e in range(experts):
        prob_send[e] = weight_rows[e:e + 1, :]
    rows[me] = send_rows[me]

    @pl.when(on_diagonal)
    def _():
        prob_recv[...] = prob_send[me]
        pl.semaphore_wait(barrier, greeted + group - 1)

    @pl.when(jnp.logical_not(on_diagonal))
    def _():
        pl.semaphore_wait(barrier, greeted)

    offsets = [(ox, oy) for ox in [None] + rx.away for oy in [None] + ry.away]
    offsets.sort(key=lambda o: -dist(o[0]) - dist(o[1]))
    place = {o: i for i, o in enumerate(offsets)}
    furthest = ring_x // 2 + ring_y // 2
    levels = (max(furthest - 2, 1), max(furthest - 3, 1), 0)
    waves = []
    for w, level in enumerate(levels):
        above = levels[w - 1] if w else furthest + 1
        waves.append([o for o in offsets if level <= dist(o[0]) + dist(o[1]) < above])

    def target(o):
        return rx.target(o[0]) * ring_y + ry.target(o[1])

    def arrived(o):
        source = target(o)

        @pl.when(source != me)
        def _():
            pltpu.make_async_remote_copy(
                send_rows.at[0], rows.at[source], disp_s.at[0], disp_r.at[source], {"expert": source}, MESH,
            ).wait_recv()

    def dispatch_copy(r):
        to = lax.rem(me + r, experts)
        return pltpu.make_async_remote_copy(
            send_rows.at[to], rows.at[me], disp_s.at[r], disp_r.at[me], {"expert": to}, MESH)

    apart_x = lax.rem(me // ring_y - rx.at + ring_x, ring_x)
    apart_y = lax.rem(lax.rem(me, ring_y) - ry.at + ring_y, ring_y)
    apart = jnp.minimum(apart_x, ring_x - apart_x) + jnp.minimum(apart_y, ring_y - apart_y)

    def prob_copy(r):
        to = lax.rem(me + r, experts)
        return pltpu.make_async_remote_copy(
            prob_send.at[to], prob_recv, prob_s.at[r], prob_r, {"expert": to}, MESH)

    @pl.when(apart >= levels[0])
    def _():
        for r in range(1, experts):
            dispatch_copy(r).start()

    for o in waves[0]:
        arrived(o)

    @pl.when(apart < levels[0])
    def _():
        for r in range(1, experts):
            dispatch_copy(r).start()

    @pl.when(on_diagonal)
    def _():
        for r in range(1, experts):
            prob_copy(r).start()

    rs_a, rs_b = rs_split
    width_a, width_b = 3 * rs_a, 3 * rs_b

    def multiply(wave):
        lo, count = place[wave[0]], len(wave)
        blk = slice(lo, lo + count)
        block = jnp.concatenate([rows[target(o)] for o in wave], axis=0)
        x, dy = block[:, 0:features], block[:, features:2 * features]
        for at, width, base in ((0, rs_a, 0), (rs_a, rs_b, width_a)):
            for c, n in pieces(width):
                for j, value in enumerate((
                    nn(x, w_gate[:, at + c:at + c + n]),
                    nn(x, w_up[:, at + c:at + c + n]),
                    nt(dy, w_down[at + c:at + c + n, :]),
                )):
                    col = base + j * width + c
                    partial[blk, :, col:col + n] = value.reshape(count, cap, n)

    for copy in loads:
        copy.wait()
    multiply(waves[0])

    plans = []
    for rings, base, width, bufs in (
        (ring_a, 0, width_a, (a1_send, a1_recv, a1_s, a1_r, a2_send, a2_recv, a2_s, a2_r)),
        (ring_b, width_a, width_b, (b1_send, b1_recv, b1_s, b1_r, b2_send, b2_recv, b2_s, b2_r)),
    ):
        first, second = rings
        inner = [None] + second.away
        one = {(o1, o2): i for i, (o1, o2) in enumerate((o1, o2) for o1 in first.away for o2 in inner)}
        two = {o2: i for i, o2 in enumerate(second.away)}
        plans.append((rings, base, width, bufs, one, two))

    def one_copy(plan, key):
        rings, _, _, bufs, one, _ = plan
        i = one[key]
        return pltpu.make_async_remote_copy(
            bufs[0].at[i], bufs[1].at[i], bufs[2].at[i], bufs[3].at[i], neighbour(rings[0], key[0][0]), MESH)

    def two_copy(plan, key):
        rings, _, _, bufs, _, two = plan
        i = two[key]
        return pltpu.make_async_remote_copy(
            bufs[4].at[i], bufs[5].at[i], bufs[6].at[i], bufs[7].at[i], neighbour(rings[1], key[0]), MESH)

    def arrived_one(plan, key, total):
        one_copy(plan, key).wait_recv()
        return total + plan[3][1][plan[4][key]].astype(F32)

    def arrived_two(plan, key, total):
        two_copy(plan, key).wait_recv()
        return total + plan[3][5][plan[5][key]]

    def own(plan, o1, o2):
        rings, base, width = plan[:3]
        return partial[place[(o1, o2) if rings[0] is rx else (o2, o1)], :, base:base + width]

    def reduced_first(plan, o2):
        total = own(plan, None, o2)
        for side in ("f", "n"):
            if plan[0][0].reach[side]:
                total = arrived_one(plan, ((side, 1), o2), total)
        return total

    for steps in range(furthest, -1, -1):
        for w in (1, 2):
            if waves[w] and steps == max(dist(o[0]) + dist(o[1]) for o in waves[w]):
                for o in waves[w]:
                    arrived(o)
                multiply(waves[w])
        if not steps:
            break
        for plan in plans:
            first, second = plan[0]
            for o1 in [None] + first.away:
                for o2 in [None] + second.away:
                    if dist(o1) + dist(o2) != steps:
                        continue
                    if o1 is not None:
                        side, t = o1
                        total = own(plan, o1, o2)
                        if t < first.reach[side]:
                            total = arrived_one(plan, ((side, t + 1), o2), total)
                        plan[3][0][plan[4][(o1, o2)]] = total.astype(BF16)
                        one_copy(plan, (o1, o2)).start()
                    else:
                        side, t = o2
                        total = reduced_first(plan, o2)
                        if t < second.reach[side]:
                            total = arrived_two(plan, (side, t + 1), total)
                        plan[3][4][plan[5][o2]] = total
                        two_copy(plan, o2).start()

    def reduced(plan):
        total = reduced_first(plan, None)
        for side in ("f", "n"):
            if plan[0][1].reach[side]:
                total = arrived_two(plan, (side, 1), total)
        return total

    @pl.when(jnp.logical_not(on_diagonal))
    def _():
        prob_copy(1).wait_recv()

    diagonal = iota((cap, 128), 0) == iota((cap, 128), 1)
    weight_col = jnp.sum(jnp.where(diagonal, prob_recv[...], 0.0), axis=1, keepdims=True)
    ag_a, ag_b = ag_split
    full_a = 3 * ag_a
    gathers = []
    for rings, base, width, sems in (
        (ring_b, 0, full_a, (ga_s, ga_r)), (ring_a, full_a, 3 * ag_b, (gb_s, gb_r))):
        first, second = rings
        keys = [("1", o1) for o1 in first.away]
        keys += [("2", o1, o2) for o1 in [None] + first.away for o2 in second.away]
        gathers.append((rings, base, width, sems, {k: i for i, k in enumerate(keys)}))

    def gather_copy(plan, key):
        rings, base, width, sems, index = plan
        if key[0] == "1":
            side, t = key[1]
            before = (side, t - 1) if t > 1 else None
            blk = block_at(rings[0].origin(before), rings[1].at, rings)
            to = neighbour(rings[0], side)
        else:
            side, t = key[2]
            before = (side, t - 1) if t > 1 else None
            blk = block_at(rings[0].origin(key[1]), rings[1].origin(before), rings)
            to = neighbour(rings[1], side)
        ref = gathered.at[blk, :, base:base + width]
        i = index[key]
        return pltpu.make_async_remote_copy(ref, ref, sems[0].at[i], sems[1].at[i], to, MESH)

    def gather_wait(plan, key):
        rings, base, width, sems, index = plan
        if key[0] == "1":
            blk = block_at(rings[0].origin(key[1]), rings[1].at, rings)
            to = neighbour(rings[0], key[1][0])
        else:
            blk = block_at(rings[0].origin(key[1]), rings[1].origin(key[2]), rings)
            to = neighbour(rings[1], key[2][0])
        ref = gathered.at[blk, :, base:base + width]
        i = index[key]
        pltpu.make_async_remote_copy(ref, ref, sems[0].at[i], sems[1].at[i], to, MESH).wait_recv()

    def onward(plan, o1):
        for side in ("f", "n"):
            if plan[0][1].reach[side]:
                gather_copy(plan, ("2", o1, (side, 1))).start()

    def gather_step(steps):
        for plan in gathers:
            first, second = plan[0]
            for o1 in [None] + first.away:
                for o2 in [None] + second.away:
                    if dist(o1) + dist(o2) != steps:
                        continue
                    if o2 is None:
                        side, t = o1
                        gather_wait(plan, ("1", o1))
                        if t < first.reach[side]:
                            gather_copy(plan, ("1", (side, t + 1))).start()
                        onward(plan, o1)
                    else:
                        side, t = o2
                        gather_wait(plan, ("2", o1, o2))
                        if t < second.reach[side]:
                            gather_copy(plan, ("2", o1, (side, t + 1))).start()

    def begin(plan):
        for side in ("f", "n"):
            if plan[0][0].reach[side]:
                gather_copy(plan, ("1", (side, 1))).start()
        onward(plan, None)

    grad_weight = jnp.zeros((cap, 1), F32)
    for which, at, width in ((0, 0, rs_a), (1, rs_a, rs_b)):
        total = reduced(plans[which])
        gate, up, bk = (total[:, j * width:(j + 1) * width] for j in range(3))
        sig = jax.nn.sigmoid(gate)
        active = gate * sig
        product = active * up
        grad_weight = grad_weight + jnp.sum(bk * product, axis=1, keepdims=True)
        scaled = weight_col * bk
        results = (
            (weight_col * product).astype(BF16),
            (scaled * up * sig * (1.0 + gate * (1.0 - sig))).astype(BF16),
            (scaled * active).astype(BF16),
        )
        for j, value in enumerate(results):
            for lo, hi, start, n in ((0, ag_a, 0, ag_a), (ag_a, ag_a + ag_b, full_a, ag_b)):
                a, b = max(lo, at), min(hi, at + width)
                if a < b:
                    col = start + j * n + a - lo
                    gathered[mine, :, col:col + b - a] = value[:, a - at:b - at]
        for part, n in ((0, ag_a), (1, ag_a + ag_b)):
            if at < n <= at + width:
                begin(gathers[part])

    rounded = grad_weight.astype(BF16).astype(F32)
    dp_send[...] = jnp.sum(jnp.where(diagonal, rounded, 0.0), axis=0, keepdims=True)

    def dp_copy(slot, where):
        return pltpu.make_async_remote_copy(
            dp_send, dp_recv.at[slot], dp_s, dp_r.at[slot], {"expert": where}, MESH)

    @pl.when(jnp.logical_not(on_diagonal))
    def _():
        dp_copy(me, mine).start()

    for r in range(1, experts):
        dispatch_copy(r).wait_send()
    for rows_of in range(group // 8):
        x = rows[rows_of * 8:rows_of * 8 + 8]
        x_t[:, rows_of * 8 * cap:(rows_of + 1) * 8 * cap] = (
            x[:, :, 0:features].reshape(8 * cap, features).astype(F32).T.astype(BF16))
        dy_t[:, rows_of * 8 * cap:(rows_of + 1) * 8 * cap] = (
            x[:, :, features:2 * features].reshape(8 * cap, features).astype(F32).T.astype(BF16))
    gather_step(1)
    gather_step(2)

    def spread_copy(r):
        return pltpu.make_async_remote_copy(
            spread, spread, bc_s.at[r], bc_r, {"dp": lax.rem(me + r, group)}, MESH)

    @pl.when(on_diagonal)
    def _():
        for r in range(1, experts):
            prob_copy(r).wait_send()
            dp_copy(lax.rem(me + r, experts), lax.rem(me + r, experts)).wait_recv()
        dp_recv[me] = dp_send[...]
        values = dp_recv[...].reshape(experts, 128).astype(BF16)
        lane = iota((tok, 128), 1)
        ids_col = nt(eye_t, ids_t.astype(BF16))
        result = jnp.zeros((tok, 128), F32)
        for k in range(top):
            pick = jnp.where(ids_col[:, k:k + 1] == iota((tok, experts), 1).astype(F32), 1.0, 0.0)
            row = nn(pick.astype(BF16), values)
            place = jnp.sum(jnp.where(pick > 0.5, rank_t, 0.0), axis=1, keepdims=True)
            found = jnp.sum(jnp.where(lane.astype(F32) == place, row, 0.0), axis=1, keepdims=True)
            result = jnp.where(lane == k, found, result)
        eye = jnp.where(iota((16, 128), 0) == iota((16, 128), 1), 1.0, 0.0).astype(BF16)
        spread[...] = jnp.zeros_like(spread)
        spread[:, 0:tok] = nt(eye, result.astype(BF16)).astype(BF16)
        for r in range(1, group):
            spread_copy(r).start()

    def source(o):
        return rx.origin(o[0]) * ring_y + ry.origin(o[1])

    def return_copy(i, to):
        return pltpu.make_async_remote_copy(
            dx_send.at[i], back.at[me], ret_s.at[i], ret_r.at[me], {"expert": to}, MESH)

    def send_home(low, high):
        wave = [o for o in offsets if low <= dist(o[0]) + dist(o[1]) <= high]
        lo, count = place[wave[0]], len(wave)
        total = jnp.zeros((count * cap, features), F32)
        for part, (at, n) in enumerate(((0, ag_a), (ag_a, ag_b))):
            for j, w in ((1, w_gate), (2, w_up)):
                begin_at = (0, full_a)[part] + j * n
                left = jnp.concatenate([gathered[source(o), :, begin_at:begin_at + n] for o in wave], axis=0)
                total = total + nt(left, w[:, at:at + n])
        dx_send[lo:lo + count] = total.astype(BF16).reshape(count, cap, features)
        for i in range(lo, lo + count):
            to = source(offsets[i])

            @pl.when(to != me)
            def _():
                return_copy(i, to).start()

            @pl.when(to == me)
            def _():
                back[me] = dx_send[i]

    bounds = SENDS
    sent = -1
    for steps in range(3, furthest + 1):
        gather_step(steps)
        if steps in bounds or steps == furthest:
            send_home(sent + 1, steps)
            sent = steps

    for part, (at, n) in enumerate(((0, ag_a), (ag_a, ag_b))):
        for c, m in pieces(n):
            start = (0, full_a)[part] + c
            for j, (left, out) in enumerate(((dy_t, g_down), (x_t, g_gate), (x_t, g_up))):
                right = gathered[:, :, start + j * n:start + j * n + m].reshape(slots, m)
                value = nn(left[...], right)
                if j == 0:
                    out[at + c:at + c + m, :] = value.T
                else:
                    out[:, at + c:at + c + m] = value
    stores = [
        pltpu.make_async_copy(src, dst, store_s.at[i])
        for i, (src, dst) in enumerate(((g_gate, o_gate), (g_up, o_up), (g_down, o_down)))
    ]
    for copy in stores:
        copy.start()

    @pl.when(jnp.logical_not(on_diagonal))
    def _():
        spread_copy(1).wait_recv()
        dp_copy(me, mine).wait_send()

    @pl.when(on_diagonal)
    def _():
        for r in range(1, group):
            spread_copy(r).wait_send()

    o_probs[...] = spread[0:top, 0:tok]
    for plan in plans:
        for key in plan[4]:
            one_copy(plan, key).wait_send()
        for key in plan[5]:
            two_copy(plan, key).wait_send()
    for plan in gathers:
        for key in plan[4]:
            gather_copy(plan, key).wait_send()
    for r in range(1, experts):
        sender = lax.rem(me + r, experts)
        pltpu.make_async_remote_copy(
            dx_send.at[0], back.at[sender], ret_s.at[0], ret_r.at[sender], {"expert": sender}, MESH).wait_recv()
    o_tokens[...] = nn(hot_t[...], back[...].reshape(slots, features)).astype(BF16)
    for i, o in enumerate(offsets):
        to = source(o)

        @pl.when(to != me)
        def _():
            return_copy(i, to).wait_send()
    for copy in stores:
        copy.wait()


def carry(parts, *refs):
    ins, outs, held, in_s, out_s = refs[:5], refs[5:10], refs[10:15], refs[15], refs[16]
    reads, writes = [], []
    for src, dst, mid in zip(ins, outs, held):
        rows = src.shape[0]
        cuts = parts if rows > 32 else 1
        for c in range(cuts):
            at, i = slice(c * rows // cuts, (c + 1) * rows // cuts), len(reads)
            reads.append(pltpu.make_async_copy(src.at[at], mid.at[at], in_s.at[i]))
            writes.append(pltpu.make_async_copy(mid.at[at], dst.at[at], out_s.at[i]))
    for copy in reads:
        copy.start()
    for read, write in zip(reads, writes):
        read.wait()
        write.start()
    for copy in writes:
        copy.wait()


def per_device(tokens, grad_out, expert_ids, probs, gate_weight, up_weight, down_weight):
    tok, features = tokens.shape
    top = expert_ids.shape[1]
    hidden = gate_weight.shape[2]
    experts, group = lax.axis_size("expert"), lax.axis_size("dp")
    cap = min(tok, 2 * tok * top // experts)
    ring_x, ring_y = RING_X, group // RING_X
    slots = experts * cap
    wide_a, wide_b = 3 * RS_SPLIT[0], 3 * RS_SPLIT[1]
    n_a1, n_a2 = (ring_x - 1) * ring_y, ring_y - 1
    n_b1, n_b2 = (ring_y - 1) * ring_x, ring_x - 1
    vmem = pltpu.VMEM
    dma = pltpu.SemaphoreType.DMA
    buffers = [
        vmem((features, hidden), BF16), vmem((features, hidden), BF16), vmem((hidden, features), BF16),
        vmem((features, hidden), F32), vmem((features, hidden), F32), vmem((hidden, features), F32),
        vmem((slots, tok), BF16), vmem((tok, slots), BF16),
        vmem((experts, cap, 2 * features), BF16), vmem((experts, cap, 2 * features), BF16),
        vmem((features, slots), BF16), vmem((features, slots), BF16),
        vmem((experts, 1, 128), F32), vmem((1, 128), F32),
        vmem((group, cap, 3 * hidden), F32),
        vmem((n_a1, cap, wide_a), BF16), vmem((n_a1, cap, wide_a), BF16),
        vmem((n_a2, cap, wide_a), F32), vmem((n_a2, cap, wide_a), F32),
        vmem((n_b1, cap, wide_b), BF16), vmem((n_b1, cap, wide_b), BF16),
        vmem((n_b2, cap, wide_b), F32), vmem((n_b2, cap, wide_b), F32),
        vmem((group, cap, 3 * hidden), BF16),
        vmem((experts, cap, features), BF16), vmem((experts, cap, features), BF16),
        vmem((1, 128), F32), vmem((experts, 1, 128), F32), vmem((16, 128), BF16),
    ]
    sems = [
        dma((3,)), dma((3,)),
        dma((experts,)), dma((experts,)), dma((experts,)), dma(()),
        dma((n_a1,)), dma((n_a1,)), dma((n_a2,)), dma((n_a2,)),
        dma((n_b1,)), dma((n_b1,)), dma((n_b2,)), dma((n_b2,)),
        dma((n_b2 * ring_y + n_a2,)), dma((n_b2 * ring_y + n_a2,)),
        dma((n_a2 * ring_x + n_b2,)), dma((n_a2 * ring_x + n_b2,)),
        dma((experts,)), dma((experts,)), dma(()), dma((experts,)), dma((group,)), dma(()),
    ]
    flops = 2 * slots * features * hidden * 8
    out = pl.pallas_call(
        functools.partial(kernel, ring_x, ring_y, cap, RS_SPLIT, AG_SPLIT),
        out_shape=(
            jax.ShapeDtypeStruct((tok, features), BF16),
            jax.ShapeDtypeStruct((top, tok), BF16),
            jax.ShapeDtypeStruct((features, hidden), F32),
            jax.ShapeDtypeStruct((features, hidden), F32),
            jax.ShapeDtypeStruct((hidden, features), F32),
        ),
        in_specs=[pl.BlockSpec(memory_space=pltpu.VMEM)] * 4 + [pl.BlockSpec(memory_space=pl.ANY)] * 3,
        out_specs=[pl.BlockSpec(memory_space=pltpu.VMEM)] * 2 + [pl.BlockSpec(memory_space=pl.ANY)] * 3,
        scratch_shapes=buffers + sems,
        compiler_params=pltpu.CompilerParams(
            collective_id=0, has_side_effects=True, vmem_limit_bytes=58 * 1024 * 1024),
        cost_estimate=pl.CostEstimate(flops=flops, bytes_accessed=4 * 1024 * 1024, transcendentals=0),
    )(tokens, grad_out, expert_ids.T, probs.T, gate_weight[0], up_weight[0], down_weight[0])
    out = pl.pallas_call(
        functools.partial(carry, CUTS),
        out_shape=[jax.ShapeDtypeStruct(o.shape, o.dtype) for o in out],
        in_specs=[pl.BlockSpec(memory_space=pl.ANY)] * 5,
        out_specs=[pl.BlockSpec(memory_space=pl.ANY)] * 5,
        scratch_shapes=[vmem(o.shape, o.dtype) for o in out] + [dma((2 + 3 * CUTS,))] * 2,
        compiler_params=pltpu.CompilerParams(vmem_limit_bytes=58 * 1024 * 1024),
        cost_estimate=pl.CostEstimate(flops=0, bytes_accessed=5 * 1024 * 1024, transcendentals=0),
    )(*out)
    grad_tokens, grad_probs, grad_gate, grad_up, grad_down = out
    return grad_tokens, grad_probs.T, grad_gate[None], grad_up[None], grad_down[None]


def solution(mesh):
    return jax.shard_map(
        per_device,
        mesh=mesh,
        in_specs=(
            P("expert", "dp"),
            P("expert", "dp"),
            P("expert", None),
            P("expert", None),
            P("expert", "dp", None),
            P("expert", "dp", None),
            P("expert", None, "dp"),
        ),
        out_specs=(
            P("expert", "dp"),
            P("expert", None),
            P("expert", "dp", None),
            P("expert", "dp", None),
            P("expert", None, "dp"),
        ),
        check_vma=False,
    )
```

```python
import functools

import jax
import jax.numpy as jnp
from jax import lax
from jax.experimental import pallas as pl
from jax.experimental.pallas import tpu as pltpu
from jax.sharding import PartitionSpec as P

MESH = pl.DeviceIdType.MESH
F32, BF16 = jnp.float32, jnp.bfloat16
RING_X = 4
RS_SPLIT = (896, 640)
AG_SPLIT = (896, 640)
SENDS = (3, 4, 5)
CUTS = 2


def nt(a, b):
    return lax.dot_general(a, b, (((1,), (1,)), ((), ())), preferred_element_type=F32)


def nn(a, b):
    return jnp.dot(a, b, preferred_element_type=F32)


def iota(shape, dim):
    return lax.broadcasted_iota(jnp.int32, shape, dim)


def pieces(width, step=256):
    return [(c, min(step, width - c)) for c in range(0, width, step)]


class Ring:
    def __init__(self, at, size, turn):
        self.at, self.size, self.turn = at, size, turn
        half = size // 2
        self.reach = {"f": half, "n": size - 1 - half}
        self.away = [("f", t) for t in range(1, half + 1)]
        self.away += [("n", t) for t in range(1, size - half)]

    def shift(self, hops):
        return lax.rem(self.at + self.turn * hops + 2 * self.size, self.size)

    def target(self, offset):
        if offset is None:
            return self.at
        side, t = offset
        return self.shift(-t if side == "f" else t)

    def origin(self, offset):
        if offset is None:
            return self.at
        side, t = offset
        return self.shift(t if side == "f" else -t)

    def following(self, side):
        return self.shift(-1 if side == "f" else 1)


def dist(offset):
    return 0 if offset is None else offset[1]


def kernel(ring_x, ring_y, cap, rs_split, ag_split, tokens, grad_out, ids, probs, h_gate, h_up, h_down,
           o_tokens, o_probs, o_gate, o_up, o_down,
           w_gate, w_up, w_down, g_gate, g_up, g_down,
           hot, hot_t, send_rows, rows, x_t, dy_t, prob_send, prob_recv, partial,
           a1_send, a1_recv, a2_send, a2_recv, a3_send, a3_recv, b1_send, b1_recv, b2_send, b2_recv,
           gathered, dx_send, back, dp_send, dp_recv, spread,
           load_s, store_s, disp_s, disp_r, prob_s, prob_r, a1_s, a1_r, a2_s, a2_r, b1_s, b1_r, b2_s, b2_r,
           ga_s, ga_r, gb_s, gb_r, ret_s, ret_r, dp_s, dp_r, bc_s, bc_r):
    me, mine = lax.axis_index("expert"), lax.axis_index("dp")
    experts, group = lax.axis_size("expert"), ring_x * ring_y
    tok, features = tokens.shape
    top = ids.shape[0]
    slots = experts * cap
    turn = 1 - 2 * lax.rem(me, 2)
    rx = Ring(mine // ring_y, ring_x, turn)
    ry = Ring(lax.rem(mine, ring_y), ring_y, turn)
    ring_a, ring_b = (rx, ry), (ry, rx)

    def block_at(first, second, rings):
        bx, by = (first, second) if rings[0] is rx else (second, first)
        return bx * ring_y + by

    def neighbour(ring, side):
        to = ring.following(side)
        return {"dp": to * ring_y + ry.at} if ring is rx else {"dp": rx.at * ring_y + to}

    barrier = pltpu.get_barrier_semaphore()

    def greet(where):
        pl.semaphore_signal(barrier, inc=1, device_id=where, device_id_type=MESH)

    for r in range(1, experts):
        greet({"expert": lax.rem(me + r, experts)})
    greeted = experts - 1
    for ring in (rx, ry):
        for side in ("f", "n"):
            if ring.reach[side]:
                greet(neighbour(ring, side))
                greeted += 1
    on_diagonal = me == mine

    @pl.when(jnp.logical_not(on_diagonal))
    def _():
        greet({"dp": me})

    loads = [
        pltpu.make_async_copy(src, dst, load_s.at[i])
        for i, (src, dst) in enumerate(((h_gate, w_gate), (h_up, w_up), (h_down, w_down)))
    ]
    for copy in loads:
        copy.start()

    ids_t = ids[...].astype(F32)
    probs_t = probs[...].astype(F32)
    expert_row = iota((experts, tok), 0).astype(F32)
    chosen = jnp.zeros((experts, tok), F32)
    weight = jnp.zeros((experts, tok), F32)
    for k in range(top):
        hit = ids_t[k:k + 1, :] == expert_row
        chosen = chosen + jnp.where(hit, 1.0, 0.0)
        weight = weight + jnp.where(hit, probs_t[k:k + 1, :], 0.0)
    earlier = jnp.where(iota((tok, tok), 0) < iota((tok, tok), 1), 1.0, 0.0).astype(BF16)
    rank = jnp.where(chosen > 0.5, nn(chosen.astype(BF16), earlier), 128.0).astype(BF16)
    owner = jnp.where(iota((slots, experts), 0) // cap == iota((slots, experts), 1), 1.0, 0.0).astype(BF16)
    owner_t = jnp.where(iota((experts, slots), 1) // cap == iota((experts, slots), 0), 1.0, 0.0).astype(BF16)
    slot_col = lax.rem(iota((slots, tok), 0), cap).astype(F32)
    slot_row = lax.rem(iota((tok, slots), 1), cap).astype(F32)
    one_hot = jnp.where(nn(owner, rank) == slot_col, 1.0, 0.0)
    hot[...] = one_hot.astype(BF16)
    eye_t = jnp.where(iota((tok, tok), 0) == iota((tok, tok), 1), 1.0, 0.0).astype(BF16)
    rank_t = nt(eye_t, rank)
    hot_t[...] = jnp.where(nn(rank_t.astype(BF16), owner_t) == slot_row, 1.0, 0.0).astype(BF16)
    send_rows[:, :, 0:features] = nn(hot[...], tokens[...]).astype(BF16).reshape(experts, cap, features)
    send_rows[:, :, features:2 * features] = nn(hot[...], grad_out[...]).astype(BF16).reshape(experts, cap, features)
    slot_weight = jnp.sum(one_hot * nn(owner, weight.astype(BF16)), axis=1, keepdims=True)
    lane_slot = iota((slots, 128), 1) == lax.rem(iota((slots, 128), 0), cap)
    weight_rows = nn(owner_t, jnp.where(lane_slot, slot_weight, 0.0).astype(BF16))
    for e in range(experts):
        prob_send[e] = weight_rows[e:e + 1, :]
    rows[me] = send_rows[me]

    @pl.when(on_diagonal)
    def _():
        prob_recv[...] = prob_send[me]
        pl.semaphore_wait(barrier, greeted + group - 1)

    @pl.when(jnp.logical_not(on_diagonal))
    def _():
        pl.semaphore_wait(barrier, greeted)

    offsets = [(ox, oy) for ox in [None] + rx.away for oy in [None] + ry.away]
    offsets.sort(key=lambda o: -dist(o[0]) - dist(o[1]))
    place = {o: i for i, o in enumerate(offsets)}
    furthest = ring_x // 2 + ring_y // 2
    levels = (max(furthest - 2, 1), max(furthest - 3, 1), 0)
    waves = []
    for w, level in enumerate(levels):
        above = levels[w - 1] if w else furthest + 1
        waves.append([o for o in offsets if level <= dist(o[0]) + dist(o[1]) < above])

    def target(o):
        return rx.target(o[0]) * ring_y + ry.target(o[1])

    def arrived(o):
        source = target(o)

        @pl.when(source != me)
        def _():
            pltpu.make_async_remote_copy(
                send_rows.at[0], rows.at[source], disp_s.at[0], disp_r.at[source], {"expert": source}, MESH,
            ).wait_recv()

    def dispatch_copy(r):
        to = lax.rem(me + r, experts)
        return pltpu.make_async_remote_copy(
            send_rows.at[to], rows.at[me], disp_s.at[r], disp_r.at[me], {"expert": to}, MESH)

    apart_x = lax.rem(me // ring_y - rx.at + ring_x, ring_x)
    apart_y = lax.rem(lax.rem(me, ring_y) - ry.at + ring_y, ring_y)
    apart = jnp.minimum(apart_x, ring_x - apart_x) + jnp.minimum(apart_y, ring_y - apart_y)

    def prob_copy(r):
        to = lax.rem(me + r, experts)
        return pltpu.make_async_remote_copy(
            prob_send.at[to], prob_recv, prob_s.at[r], prob_r, {"expert": to}, MESH)

    @pl.when(apart >= levels[0])
    def _():
        for r in range(1, experts):
            dispatch_copy(r).start()

    for o in waves[0]:
        arrived(o)

    @pl.when(apart < levels[0])
    def _():
        for r in range(1, experts):
            dispatch_copy(r).start()

    @pl.when(on_diagonal)
    def _():
        for r in range(1, experts):
            prob_copy(r).start()

    rs_a, rs_b = rs_split
    width_a, width_b = 3 * rs_a, 3 * rs_b

    def multiply(wave):
        lo, count = place[wave[0]], len(wave)
        blk = slice(lo, lo + count)
        block = jnp.concatenate([rows[target(o)] for o in wave], axis=0)
        x, dy = block[:, 0:features], block[:, features:2 * features]
        for at, width, base in ((0, rs_a, 0), (rs_a, rs_b, width_a)):
            for c, n in pieces(width):
                for j, value in enumerate((
                    nn(x, w_gate[:, at + c:at + c + n]),
                    nn(x, w_up[:, at + c:at + c + n]),
                    nt(dy, w_down[at + c:at + c + n, :]),
                )):
                    col = base + j * width + c
                    partial[blk, :, col:col + n] = value.reshape(count, cap, n)

    for copy in loads:
        copy.wait()
    multiply(waves[0])

    plans = []
    for rings, base, width, bufs in (
        (ring_a, 0, width_a, (a1_send, a1_recv, a1_s, a1_r, a2_send, a2_recv, a2_s, a2_r, a3_send, a3_recv)),
        (ring_b, width_a, width_b, (b1_send, b1_recv, b1_s, b1_r, b2_send, b2_recv, b2_s, b2_r)),
    ):
        first, second = rings
        inner = [None] + second.away
        one = {(o1, o2): i for i, (o1, o2) in enumerate((o1, o2) for o1 in first.away for o2 in inner)}
        two = {o2: i for i, o2 in enumerate(second.away)}
        plans.append((rings, base, width, bufs, one, two))

    def one_copy(plan, key):
        rings, _, _, bufs, one, _ = plan
        i = one[key]
        return pltpu.make_async_remote_copy(
            bufs[0].at[i], bufs[1].at[i], bufs[2].at[i], bufs[3].at[i], neighbour(rings[0], key[0][0]), MESH)

    def sides(plan, key):
        bufs = plan[3]
        early = plan[0][1].reach[key[0]] - key[1] < 2
        return bufs[8:10] if len(bufs) > 8 and early else bufs[4:6]

    def two_copy(plan, key):
        rings, _, _, bufs, _, two = plan
        i = two[key]
        src, dst = sides(plan, key)
        return pltpu.make_async_remote_copy(
            src.at[i], dst.at[i], bufs[6].at[i], bufs[7].at[i], neighbour(rings[1], key[0]), MESH)

    def arrived_one(plan, key, total):
        one_copy(plan, key).wait_recv()
        return total + plan[3][1][plan[4][key]].astype(F32)

    def arrived_two(plan, key, total):
        two_copy(plan, key).wait_recv()
        return total + sides(plan, key)[1][plan[5][key]].astype(F32)

    def own(plan, o1, o2):
        rings, base, width = plan[:3]
        return partial[place[(o1, o2) if rings[0] is rx else (o2, o1)], :, base:base + width]

    def reduced_first(plan, o2):
        total = own(plan, None, o2)
        for side in ("f", "n"):
            if plan[0][0].reach[side]:
                total = arrived_one(plan, ((side, 1), o2), total)
        return total

    for steps in range(furthest, -1, -1):
        for w in (1, 2):
            if waves[w] and steps == max(dist(o[0]) + dist(o[1]) for o in waves[w]):
                for o in waves[w]:
                    arrived(o)
                multiply(waves[w])
        if not steps:
            break
        for plan in plans:
            first, second = plan[0]
            for o1 in [None] + first.away:
                for o2 in [None] + second.away:
                    if dist(o1) + dist(o2) != steps:
                        continue
                    if o1 is not None:
                        side, t = o1
                        total = own(plan, o1, o2)
                        if t < first.reach[side]:
                            total = arrived_one(plan, ((side, t + 1), o2), total)
                        plan[3][0][plan[4][(o1, o2)]] = total.astype(BF16)
                        one_copy(plan, (o1, o2)).start()
                    else:
                        side, t = o2
                        total = reduced_first(plan, o2)
                        if t < second.reach[side]:
                            total = arrived_two(plan, (side, t + 1), total)
                        store = sides(plan, o2)[0]
                        store[plan[5][o2]] = total.astype(store.dtype)
                        two_copy(plan, o2).start()

    def reduced(plan):
        total = reduced_first(plan, None)
        for side in ("f", "n"):
            if plan[0][1].reach[side]:
                total = arrived_two(plan, (side, 1), total)
        return total

    @pl.when(jnp.logical_not(on_diagonal))
    def _():
        prob_copy(1).wait_recv()

    diagonal = iota((cap, 128), 0) == iota((cap, 128), 1)
    weight_col = jnp.sum(jnp.where(diagonal, prob_recv[...], 0.0), axis=1, keepdims=True)
    ag_a, ag_b = ag_split
    full_a = 3 * ag_a
    gathers = []
    for rings, base, width, sems in (
        (ring_b, 0, full_a, (ga_s, ga_r)), (ring_a, full_a, 3 * ag_b, (gb_s, gb_r))):
        first, second = rings
        keys = [("1", o1) for o1 in first.away]
        keys += [("2", o1, o2) for o1 in [None] + first.away for o2 in second.away]
        gathers.append((rings, base, width, sems, {k: i for i, k in enumerate(keys)}))

    def gather_copy(plan, key):
        rings, base, width, sems, index = plan
        if key[0] == "1":
            side, t = key[1]
            before = (side, t - 1) if t > 1 else None
            blk = block_at(rings[0].origin(before), rings[1].at, rings)
            to = neighbour(rings[0], side)
        else:
            side, t = key[2]
            before = (side, t - 1) if t > 1 else None
            blk = block_at(rings[0].origin(key[1]), rings[1].origin(before), rings)
            to = neighbour(rings[1], side)
        ref = gathered.at[blk, :, base:base + width]
        i = index[key]
        return pltpu.make_async_remote_copy(ref, ref, sems[0].at[i], sems[1].at[i], to, MESH)

    def gather_wait(plan, key):
        rings, base, width, sems, index = plan
        if key[0] == "1":
            blk = block_at(rings[0].origin(key[1]), rings[1].at, rings)
            to = neighbour(rings[0], key[1][0])
        else:
            blk = block_at(rings[0].origin(key[1]), rings[1].origin(key[2]), rings)
            to = neighbour(rings[1], key[2][0])
        ref = gathered.at[blk, :, base:base + width]
        i = index[key]
        pltpu.make_async_remote_copy(ref, ref, sems[0].at[i], sems[1].at[i], to, MESH).wait_recv()

    def onward(plan, o1):
        for side in ("f", "n"):
            if plan[0][1].reach[side]:
                gather_copy(plan, ("2", o1, (side, 1))).start()

    def gather_step(steps):
        for plan in gathers:
            first, second = plan[0]
            for o1 in [None] + first.away:
                for o2 in [None] + second.away:
                    if dist(o1) + dist(o2) != steps:
                        continue
                    if o2 is None:
                        side, t = o1
                        gather_wait(plan, ("1", o1))
                        if t < first.reach[side]:
                            gather_copy(plan, ("1", (side, t + 1))).start()
                        onward(plan, o1)
                    else:
                        side, t = o2
                        gather_wait(plan, ("2", o1, o2))
                        if t < second.reach[side]:
                            gather_copy(plan, ("2", o1, (side, t + 1))).start()

    def begin(plan):
        for side in ("f", "n"):
            if plan[0][0].reach[side]:
                gather_copy(plan, ("1", (side, 1))).start()
        onward(plan, None)

    grad_weight = jnp.zeros((cap, 1), F32)
    for which, at, width in ((0, 0, rs_a), (1, rs_a, rs_b)):
        total = reduced(plans[which])
        gate, up, bk = (total[:, j * width:(j + 1) * width] for j in range(3))
        sig = jax.nn.sigmoid(gate)
        active = gate * sig
        product = active * up
        grad_weight = grad_weight + jnp.sum(bk * product, axis=1, keepdims=True)
        scaled = weight_col * bk
        results = (
            (weight_col * product).astype(BF16),
            (scaled * up * sig * (1.0 + gate * (1.0 - sig))).astype(BF16),
            (scaled * active).astype(BF16),
        )
        for j, value in enumerate(results):
            for lo, hi, start, n in ((0, ag_a, 0, ag_a), (ag_a, ag_a + ag_b, full_a, ag_b)):
                a, b = max(lo, at), min(hi, at + width)
                if a < b:
                    col = start + j * n + a - lo
                    gathered[mine, :, col:col + b - a] = value[:, a - at:b - at]
        for part, n in ((0, ag_a), (1, ag_a + ag_b)):
            if at < n <= at + width:
                begin(gathers[part])

    rounded = grad_weight.astype(BF16).astype(F32)
    dp_send[...] = jnp.sum(jnp.where(diagonal, rounded, 0.0), axis=0, keepdims=True)

    def dp_copy(slot, where):
        return pltpu.make_async_remote_copy(
            dp_send, dp_recv.at[slot], dp_s, dp_r.at[slot], {"expert": where}, MESH)

    @pl.when(jnp.logical_not(on_diagonal))
    def _():
        dp_copy(me, mine).start()

    for r in range(1, experts):
        dispatch_copy(r).wait_send()
    for rows_of in range(group // 8):
        x = rows[rows_of * 8:rows_of * 8 + 8]
        x_t[:, rows_of * 8 * cap:(rows_of + 1) * 8 * cap] = (
            x[:, :, 0:features].reshape(8 * cap, features).astype(F32).T.astype(BF16))
        dy_t[:, rows_of * 8 * cap:(rows_of + 1) * 8 * cap] = (
            x[:, :, features:2 * features].reshape(8 * cap, features).astype(F32).T.astype(BF16))
    gather_step(1)
    gather_step(2)

    def spread_copy(r):
        return pltpu.make_async_remote_copy(
            spread, spread, bc_s.at[r], bc_r, {"dp": lax.rem(me + r, group)}, MESH)

    @pl.when(on_diagonal)
    def _():
        for r in range(1, experts):
            prob_copy(r).wait_send()
            dp_copy(lax.rem(me + r, experts), lax.rem(me + r, experts)).wait_recv()
        dp_recv[me] = dp_send[...]
        values = dp_recv[...].reshape(experts, 128).astype(BF16)
        lane = iota((tok, 128), 1)
        ids_col = nt(eye_t, ids_t.astype(BF16))
        result = jnp.zeros((tok, 128), F32)
        for k in range(top):
            pick = jnp.where(ids_col[:, k:k + 1] == iota((tok, experts), 1).astype(F32), 1.0, 0.0)
            row = nn(pick.astype(BF16), values)
            place = jnp.sum(jnp.where(pick > 0.5, rank_t, 0.0), axis=1, keepdims=True)
            found = jnp.sum(jnp.where(lane.astype(F32) == place, row, 0.0), axis=1, keepdims=True)
            result = jnp.where(lane == k, found, result)
        eye = jnp.where(iota((16, 128), 0) == iota((16, 128), 1), 1.0, 0.0).astype(BF16)
        spread[...] = jnp.zeros_like(spread)
        spread[:, 0:tok] = nt(eye, result.astype(BF16)).astype(BF16)
        for r in range(1, group):
            spread_copy(r).start()

    def source(o):
        return rx.origin(o[0]) * ring_y + ry.origin(o[1])

    def return_copy(i, to):
        return pltpu.make_async_remote_copy(
            dx_send.at[i], back.at[me], ret_s.at[i], ret_r.at[me], {"expert": to}, MESH)

    def send_home(low, high):
        wave = [o for o in offsets if low <= dist(o[0]) + dist(o[1]) <= high]
        lo, count = place[wave[0]], len(wave)
        total = jnp.zeros((count * cap, features), F32)
        for part, (at, n) in enumerate(((0, ag_a), (ag_a, ag_b))):
            for j, w in ((1, w_gate), (2, w_up)):
                begin_at = (0, full_a)[part] + j * n
                left = jnp.concatenate([gathered[source(o), :, begin_at:begin_at + n] for o in wave], axis=0)
                total = total + nt(left, w[:, at:at + n])
        dx_send[lo:lo + count] = total.astype(BF16).reshape(count, cap, features)
        for i in range(lo, lo + count):
            to = source(offsets[i])

            @pl.when(to != me)
            def _():
                return_copy(i, to).start()

            @pl.when(to == me)
            def _():
                back[me] = dx_send[i]

    bounds = SENDS
    sent = -1
    for steps in range(3, furthest + 1):
        gather_step(steps)
        if steps in bounds or steps == furthest:
            send_home(sent + 1, steps)
            sent = steps

    for part, (at, n) in enumerate(((0, ag_a), (ag_a, ag_b))):
        for c, m in pieces(n):
            start = (0, full_a)[part] + c
            for j, (left, out) in enumerate(((dy_t, g_down), (x_t, g_gate), (x_t, g_up))):
                right = gathered[:, :, start + j * n:start + j * n + m].reshape(slots, m)
                value = nn(left[...], right)
                if j == 0:
                    out[at + c:at + c + m, :] = value.T
                else:
                    out[:, at + c:at + c + m] = value
    stores = [
        pltpu.make_async_copy(src, dst, store_s.at[i])
        for i, (src, dst) in enumerate(((g_gate, o_gate), (g_up, o_up), (g_down, o_down)))
    ]
    for copy in stores:
        copy.start()

    @pl.when(jnp.logical_not(on_diagonal))
    def _():
        spread_copy(1).wait_recv()
        dp_copy(me, mine).wait_send()

    @pl.when(on_diagonal)
    def _():
        for r in range(1, group):
            spread_copy(r).wait_send()

    o_probs[...] = spread[0:top, 0:tok]
    for plan in plans:
        for key in plan[4]:
            one_copy(plan, key).wait_send()
        for key in plan[5]:
            two_copy(plan, key).wait_send()
    for plan in gathers:
        for key in plan[4]:
            gather_copy(plan, key).wait_send()
    for r in range(1, experts):
        sender = lax.rem(me + r, experts)
        pltpu.make_async_remote_copy(
            dx_send.at[0], back.at[sender], ret_s.at[0], ret_r.at[sender], {"expert": sender}, MESH).wait_recv()
    o_tokens[...] = nn(hot_t[...], back[...].reshape(slots, features)).astype(BF16)
    for i, o in enumerate(offsets):
        to = source(o)

        @pl.when(to != me)
        def _():
            return_copy(i, to).wait_send()
    for copy in stores:
        copy.wait()


def carry(parts, *refs):
    ins, outs, held, in_s, out_s = refs[:5], refs[5:10], refs[10:15], refs[15], refs[16]
    reads, writes = [], []
    for src, dst, mid in zip(ins, outs, held):
        rows = src.shape[0]
        cuts = parts if rows > 32 else 1
        for c in range(cuts):
            at, i = slice(c * rows // cuts, (c + 1) * rows // cuts), len(reads)
            reads.append(pltpu.make_async_copy(src.at[at], mid.at[at], in_s.at[i]))
            writes.append(pltpu.make_async_copy(mid.at[at], dst.at[at], out_s.at[i]))
    for copy in reads:
        copy.start()
    for read, write in zip(reads, writes):
        read.wait()
        write.start()
    for copy in writes:
        copy.wait()


def per_device(tokens, grad_out, expert_ids, probs, gate_weight, up_weight, down_weight):
    tok, features = tokens.shape
    top = expert_ids.shape[1]
    hidden = gate_weight.shape[2]
    experts, group = lax.axis_size("expert"), lax.axis_size("dp")
    cap = min(tok, 2 * tok * top // experts)
    ring_x, ring_y = RING_X, group // RING_X
    slots = experts * cap
    wide_a, wide_b = 3 * RS_SPLIT[0], 3 * RS_SPLIT[1]
    n_a1, n_a2 = (ring_x - 1) * ring_y, ring_y - 1
    n_b1, n_b2 = (ring_y - 1) * ring_x, ring_x - 1
    vmem = pltpu.VMEM
    dma = pltpu.SemaphoreType.DMA
    buffers = [
        vmem((features, hidden), BF16), vmem((features, hidden), BF16), vmem((hidden, features), BF16),
        vmem((features, hidden), F32), vmem((features, hidden), F32), vmem((hidden, features), F32),
        vmem((slots, tok), BF16), vmem((tok, slots), BF16),
        vmem((experts, cap, 2 * features), BF16), vmem((experts, cap, 2 * features), BF16),
        vmem((features, slots), BF16), vmem((features, slots), BF16),
        vmem((experts, 1, 128), F32), vmem((1, 128), F32),
        vmem((group, cap, 3 * hidden), F32),
        vmem((n_a1, cap, wide_a), BF16), vmem((n_a1, cap, wide_a), BF16),
        vmem((n_a2, cap, wide_a), F32), vmem((n_a2, cap, wide_a), F32),
        vmem((n_a2, cap, wide_a), BF16), vmem((n_a2, cap, wide_a), BF16),
        vmem((n_b1, cap, wide_b), BF16), vmem((n_b1, cap, wide_b), BF16),
        vmem((n_b2, cap, wide_b), F32), vmem((n_b2, cap, wide_b), F32),
        vmem((group, cap, 3 * hidden), BF16),
        vmem((experts, cap, features), BF16), vmem((experts, cap, features), BF16),
        vmem((1, 128), F32), vmem((experts, 1, 128), F32), vmem((16, 128), BF16),
    ]
    sems = [
        dma((3,)), dma((3,)),
        dma((experts,)), dma((experts,)), dma((experts,)), dma(()),
        dma((n_a1,)), dma((n_a1,)), dma((n_a2,)), dma((n_a2,)),
        dma((n_b1,)), dma((n_b1,)), dma((n_b2,)), dma((n_b2,)),
        dma((n_b2 * ring_y + n_a2,)), dma((n_b2 * ring_y + n_a2,)),
        dma((n_a2 * ring_x + n_b2,)), dma((n_a2 * ring_x + n_b2,)),
        dma((experts,)), dma((experts,)), dma(()), dma((experts,)), dma((group,)), dma(()),
    ]
    flops = 2 * slots * features * hidden * 8
    out = pl.pallas_call(
        functools.partial(kernel, ring_x, ring_y, cap, RS_SPLIT, AG_SPLIT),
        out_shape=(
            jax.ShapeDtypeStruct((tok, features), BF16),
            jax.ShapeDtypeStruct((top, tok), BF16),
            jax.ShapeDtypeStruct((features, hidden), F32),
            jax.ShapeDtypeStruct((features, hidden), F32),
            jax.ShapeDtypeStruct((hidden, features), F32),
        ),
        in_specs=[pl.BlockSpec(memory_space=pltpu.VMEM)] * 4 + [pl.BlockSpec(memory_space=pl.ANY)] * 3,
        out_specs=[pl.BlockSpec(memory_space=pltpu.VMEM)] * 2 + [pl.BlockSpec(memory_space=pl.ANY)] * 3,
        scratch_shapes=buffers + sems,
        compiler_params=pltpu.CompilerParams(
            collective_id=0, has_side_effects=True, vmem_limit_bytes=58 * 1024 * 1024),
        cost_estimate=pl.CostEstimate(flops=flops, bytes_accessed=4 * 1024 * 1024, transcendentals=0),
    )(tokens, grad_out, expert_ids.T, probs.T, gate_weight[0], up_weight[0], down_weight[0])
    out = pl.pallas_call(
        functools.partial(carry, CUTS),
        out_shape=[jax.ShapeDtypeStruct(o.shape, o.dtype) for o in out],
        in_specs=[pl.BlockSpec(memory_space=pl.ANY)] * 5,
        out_specs=[pl.BlockSpec(memory_space=pl.ANY)] * 5,
        scratch_shapes=[vmem(o.shape, o.dtype) for o in out] + [dma((2 + 3 * CUTS,))] * 2,
        compiler_params=pltpu.CompilerParams(vmem_limit_bytes=58 * 1024 * 1024),
        cost_estimate=pl.CostEstimate(flops=0, bytes_accessed=5 * 1024 * 1024, transcendentals=0),
    )(*out)
    grad_tokens, grad_probs, grad_gate, grad_up, grad_down = out
    return grad_tokens, grad_probs.T, grad_gate[None], grad_up[None], grad_down[None]


def solution(mesh):
    return jax.shard_map(
        per_device,
        mesh=mesh,
        in_specs=(
            P("expert", "dp"),
            P("expert", "dp"),
            P("expert", None),
            P("expert", None),
            P("expert", "dp", None),
            P("expert", "dp", None),
            P("expert", None, "dp"),
        ),
        out_specs=(
            P("expert", "dp"),
            P("expert", None),
            P("expert", "dp", None),
            P("expert", "dp", None),
            P("expert", None, "dp"),
        ),
        check_vma=False,
    )
```

```python
import functools

import jax
import jax.numpy as jnp
from jax import lax
from jax.experimental import pallas as pl
from jax.experimental.pallas import tpu as pltpu
from jax.sharding import PartitionSpec as P

MESH = pl.DeviceIdType.MESH
F32, BF16 = jnp.float32, jnp.bfloat16
RING_X = 4
RS_SPLIT = (896, 640)
AG_SPLIT = (896, 640)
SENDS = (3, 4, 5)
CUTS = 2


def nt(a, b):
    return lax.dot_general(a, b, (((1,), (1,)), ((), ())), preferred_element_type=F32)


def nn(a, b):
    return jnp.dot(a, b, preferred_element_type=F32)


def iota(shape, dim):
    return lax.broadcasted_iota(jnp.int32, shape, dim)


def pieces(width, step=256):
    return [(c, min(step, width - c)) for c in range(0, width, step)]


class Ring:
    def __init__(self, at, size, turn):
        self.at, self.size, self.turn = at, size, turn
        half = size // 2
        self.reach = {"f": half, "n": size - 1 - half}
        self.away = [("f", t) for t in range(1, half + 1)]
        self.away += [("n", t) for t in range(1, size - half)]

    def shift(self, hops):
        return lax.rem(self.at + self.turn * hops + 2 * self.size, self.size)

    def target(self, offset):
        if offset is None:
            return self.at
        side, t = offset
        return self.shift(-t if side == "f" else t)

    def origin(self, offset):
        if offset is None:
            return self.at
        side, t = offset
        return self.shift(t if side == "f" else -t)

    def following(self, side):
        return self.shift(-1 if side == "f" else 1)


def dist(offset):
    return 0 if offset is None else offset[1]


def kernel(ring_x, ring_y, cap, rs_split, ag_split, tokens, grad_out, ids, probs, h_gate, h_up, h_down,
           o_tokens, o_probs, o_gate, o_up, o_down,
           w_gate, w_up, w_down, g_gate, g_up, g_down,
           hot, hot_t, send_rows, rows, x_t, dy_t, prob_send, prob_recv, partial,
           a1_send, a1_recv, a2_send, a2_recv, a3_send, a3_recv, b1_send, b1_recv, b2_send, b2_recv,
           gathered, dx_send, back, dp_send, dp_recv, spread,
           load_s, store_s, disp_s, disp_r, prob_s, prob_r, a1_s, a1_r, a2_s, a2_r, b1_s, b1_r, b2_s, b2_r,
           ga_s, ga_r, gb_s, gb_r, ret_s, ret_r, dp_s, dp_r, bc_s, bc_r):
    me, mine = lax.axis_index("expert"), lax.axis_index("dp")
    experts, group = lax.axis_size("expert"), ring_x * ring_y
    tok, features = tokens.shape
    top = ids.shape[0]
    slots = experts * cap
    turn = 1 - 2 * lax.rem(me, 2)
    rx = Ring(mine // ring_y, ring_x, turn)
    ry = Ring(lax.rem(mine, ring_y), ring_y, turn)
    ring_a, ring_b = (rx, ry), (ry, rx)

    def block_at(first, second, rings):
        bx, by = (first, second) if rings[0] is rx else (second, first)
        return bx * ring_y + by

    def neighbour(ring, side):
        to = ring.following(side)
        return {"dp": to * ring_y + ry.at} if ring is rx else {"dp": rx.at * ring_y + to}

    barrier = pltpu.get_barrier_semaphore()

    def greet(where):
        pl.semaphore_signal(barrier, inc=1, device_id=where, device_id_type=MESH)

    for r in range(1, experts):
        greet({"expert": lax.rem(me + r, experts)})
    greeted = experts - 1
    for ring in (rx, ry):
        for side in ("f", "n"):
            if ring.reach[side]:
                greet(neighbour(ring, side))
                greeted += 1
    on_diagonal = me == mine

    @pl.when(jnp.logical_not(on_diagonal))
    def _():
        greet({"dp": me})

    loads = [
        pltpu.make_async_copy(src, dst, load_s.at[i])
        for i, (src, dst) in enumerate(((h_gate, w_gate), (h_up, w_up), (h_down, w_down)))
    ]
    for copy in loads:
        copy.start()

    ids_t = ids[...].astype(F32)
    probs_t = probs[...].astype(F32)
    expert_row = iota((experts, tok), 0).astype(F32)
    chosen = jnp.zeros((experts, tok), F32)
    weight = jnp.zeros((experts, tok), F32)
    for k in range(top):
        hit = ids_t[k:k + 1, :] == expert_row
        chosen = chosen + jnp.where(hit, 1.0, 0.0)
        weight = weight + jnp.where(hit, probs_t[k:k + 1, :], 0.0)
    earlier = jnp.where(iota((tok, tok), 0) < iota((tok, tok), 1), 1.0, 0.0).astype(BF16)
    rank = jnp.where(chosen > 0.5, nn(chosen.astype(BF16), earlier), 128.0).astype(BF16)
    owner = jnp.where(iota((slots, experts), 0) // cap == iota((slots, experts), 1), 1.0, 0.0).astype(BF16)
    owner_t = jnp.where(iota((experts, slots), 1) // cap == iota((experts, slots), 0), 1.0, 0.0).astype(BF16)
    slot_col = lax.rem(iota((slots, tok), 0), cap).astype(F32)
    slot_row = lax.rem(iota((tok, slots), 1), cap).astype(F32)
    one_hot = jnp.where(nn(owner, rank) == slot_col, 1.0, 0.0)
    hot[...] = one_hot.astype(BF16)
    eye_t = jnp.where(iota((tok, tok), 0) == iota((tok, tok), 1), 1.0, 0.0).astype(BF16)
    rank_t = nt(eye_t, rank)
    hot_t[...] = jnp.where(nn(rank_t.astype(BF16), owner_t) == slot_row, 1.0, 0.0).astype(BF16)
    send_rows[:, :, 0:features] = nn(hot[...], tokens[...]).astype(BF16).reshape(experts, cap, features)
    send_rows[:, :, features:2 * features] = nn(hot[...], grad_out[...]).astype(BF16).reshape(experts, cap, features)
    slot_weight = jnp.sum(one_hot * nn(owner, weight.astype(BF16)), axis=1, keepdims=True)
    lane_slot = iota((slots, 128), 1) == lax.rem(iota((slots, 128), 0), cap)
    weight_rows = nn(owner_t, jnp.where(lane_slot, slot_weight, 0.0).astype(BF16))
    for e in range(experts):
        prob_send[e] = weight_rows[e:e + 1, :]
    rows[me] = send_rows[me]

    @pl.when(on_diagonal)
    def _():
        prob_recv[...] = prob_send[me]
        pl.semaphore_wait(barrier, greeted + group - 1)

    @pl.when(jnp.logical_not(on_diagonal))
    def _():
        pl.semaphore_wait(barrier, greeted)

    offsets = [(ox, oy) for ox in [None] + rx.away for oy in [None] + ry.away]
    offsets.sort(key=lambda o: -dist(o[0]) - dist(o[1]))
    place = {o: i for i, o in enumerate(offsets)}
    furthest = ring_x // 2 + ring_y // 2
    levels = (max(furthest - 2, 1), max(furthest - 3, 1), 0)
    waves = []
    for w, level in enumerate(levels):
        above = levels[w - 1] if w else furthest + 1
        waves.append([o for o in offsets if level <= dist(o[0]) + dist(o[1]) < above])

    def target(o):
        return rx.target(o[0]) * ring_y + ry.target(o[1])

    def arrived(o):
        source = target(o)

        @pl.when(source != me)
        def _():
            pltpu.make_async_remote_copy(
                send_rows.at[0], rows.at[source], disp_s.at[0], disp_r.at[source], {"expert": source}, MESH,
            ).wait_recv()

    def dispatch_copy(r):
        to = lax.rem(me + r, experts)
        return pltpu.make_async_remote_copy(
            send_rows.at[to], rows.at[me], disp_s.at[r], disp_r.at[me], {"expert": to}, MESH)

    apart_x = lax.rem(me // ring_y - rx.at + ring_x, ring_x)
    apart_y = lax.rem(lax.rem(me, ring_y) - ry.at + ring_y, ring_y)
    apart = jnp.minimum(apart_x, ring_x - apart_x) + jnp.minimum(apart_y, ring_y - apart_y)

    def prob_copy(r):
        to = lax.rem(me + r, experts)
        return pltpu.make_async_remote_copy(
            prob_send.at[to], prob_recv, prob_s.at[r], prob_r, {"expert": to}, MESH)

    @pl.when(apart >= levels[0])
    def _():
        for r in range(1, experts):
            dispatch_copy(r).start()

    for o in waves[0]:
        arrived(o)

    @pl.when(apart < levels[0])
    def _():
        for r in range(1, experts):
            dispatch_copy(r).start()

    @pl.when(on_diagonal)
    def _():
        for r in range(1, experts):
            prob_copy(r).start()

    rs_a, rs_b = rs_split
    width_a, width_b = 3 * rs_a, 3 * rs_b

    def multiply(wave):
        lo, count = place[wave[0]], len(wave)
        blk = slice(lo, lo + count)
        block = jnp.concatenate([rows[target(o)] for o in wave], axis=0)
        x, dy = block[:, 0:features], block[:, features:2 * features]
        for at, width, base in ((0, rs_a, 0), (rs_a, rs_b, width_a)):
            for c, n in pieces(width):
                for j, value in enumerate((
                    nn(x, w_gate[:, at + c:at + c + n]),
                    nn(x, w_up[:, at + c:at + c + n]),
                    nt(dy, w_down[at + c:at + c + n, :]),
                )):
                    col = base + j * width + c
                    partial[blk, :, col:col + n] = value.reshape(count, cap, n)

    for copy in loads:
        copy.wait()
    multiply(waves[0])

    plans = []
    for rings, base, width, bufs in (
        (ring_a, 0, width_a, (a1_send, a1_recv, a1_s, a1_r, a2_send, a2_recv, a2_s, a2_r, a3_send, a3_recv)),
        (ring_b, width_a, width_b, (b1_send, b1_recv, b1_s, b1_r, b2_send, b2_recv, b2_s, b2_r)),
    ):
        first, second = rings
        inner = [None] + second.away
        one = {(o1, o2): i for i, (o1, o2) in enumerate((o1, o2) for o1 in first.away for o2 in inner)}
        two = {o2: i for i, o2 in enumerate(second.away)}
        plans.append((rings, base, width, bufs, one, two))

    def one_copy(plan, key):
        rings, _, _, bufs, one, _ = plan
        i = one[key]
        return pltpu.make_async_remote_copy(
            bufs[0].at[i], bufs[1].at[i], bufs[2].at[i], bufs[3].at[i], neighbour(rings[0], key[0][0]), MESH)

    def sides(plan, key):
        bufs = plan[3]
        early = plan[0][1].reach[key[0]] - key[1] < 2
        return bufs[8:10] if len(bufs) > 8 and early else bufs[4:6]

    def two_copy(plan, key):
        rings, _, _, bufs, _, two = plan
        i = two[key]
        src, dst = sides(plan, key)
        return pltpu.make_async_remote_copy(
            src.at[i], dst.at[i], bufs[6].at[i], bufs[7].at[i], neighbour(rings[1], key[0]), MESH)

    def arrived_one(plan, key, total):
        one_copy(plan, key).wait_recv()
        return total + plan[3][1][plan[4][key]].astype(F32)

    def arrived_two(plan, key, total):
        two_copy(plan, key).wait_recv()
        return total + sides(plan, key)[1][plan[5][key]].astype(F32)

    def own(plan, o1, o2):
        rings, base, width = plan[:3]
        return partial[place[(o1, o2) if rings[0] is rx else (o2, o1)], :, base:base + width]

    def reduced_first(plan, o2):
        total = own(plan, None, o2)
        for side in ("f", "n"):
            if plan[0][0].reach[side]:
                total = arrived_one(plan, ((side, 1), o2), total)
        return total

    for steps in range(furthest, -1, -1):
        for w in (1, 2):
            if waves[w] and steps == max(dist(o[0]) + dist(o[1]) for o in waves[w]):
                for o in waves[w]:
                    arrived(o)
                multiply(waves[w])
        if not steps:
            break
        for plan in plans:
            first, second = plan[0]
            for o1 in [None] + first.away:
                for o2 in [None] + second.away:
                    if dist(o1) + dist(o2) != steps:
                        continue
                    if o1 is not None:
                        side, t = o1
                        total = own(plan, o1, o2)
                        if t < first.reach[side]:
                            total = arrived_one(plan, ((side, t + 1), o2), total)
                        plan[3][0][plan[4][(o1, o2)]] = total.astype(BF16)
                        one_copy(plan, (o1, o2)).start()
                    else:
                        side, t = o2
                        total = reduced_first(plan, o2)
                        if t < second.reach[side]:
                            total = arrived_two(plan, (side, t + 1), total)
                        store = sides(plan, o2)[0]
                        store[plan[5][o2]] = total.astype(store.dtype)
                        two_copy(plan, o2).start()

    def reduced(plan):
        total = reduced_first(plan, None)
        for side in ("f", "n"):
            if plan[0][1].reach[side]:
                total = arrived_two(plan, (side, 1), total)
        return total

    @pl.when(jnp.logical_not(on_diagonal))
    def _():
        prob_copy(1).wait_recv()

    diagonal = iota((cap, 128), 0) == iota((cap, 128), 1)
    weight_col = jnp.sum(jnp.where(diagonal, prob_recv[...], 0.0), axis=1, keepdims=True)
    ag_a, ag_b = ag_split
    full_a = 3 * ag_a
    gathers = []
    for rings, base, width, sems in (
        (ring_b, 0, full_a, (ga_s, ga_r)), (ring_a, full_a, 3 * ag_b, (gb_s, gb_r))):
        first, second = rings
        keys = [("1", o1) for o1 in first.away]
        keys += [("2", o1, o2) for o1 in [None] + first.away for o2 in second.away]
        gathers.append((rings, base, width, sems, {k: i for i, k in enumerate(keys)}))

    def gather_copy(plan, key):
        rings, base, width, sems, index = plan
        if key[0] == "1":
            side, t = key[1]
            before = (side, t - 1) if t > 1 else None
            blk = block_at(rings[0].origin(before), rings[1].at, rings)
            to = neighbour(rings[0], side)
        else:
            side, t = key[2]
            before = (side, t - 1) if t > 1 else None
            blk = block_at(rings[0].origin(key[1]), rings[1].origin(before), rings)
            to = neighbour(rings[1], side)
        ref = gathered.at[blk, :, base:base + width]
        i = index[key]
        return pltpu.make_async_remote_copy(ref, ref, sems[0].at[i], sems[1].at[i], to, MESH)

    def gather_wait(plan, key):
        rings, base, width, sems, index = plan
        if key[0] == "1":
            blk = block_at(rings[0].origin(key[1]), rings[1].at, rings)
            to = neighbour(rings[0], key[1][0])
        else:
            blk = block_at(rings[0].origin(key[1]), rings[1].origin(key[2]), rings)
            to = neighbour(rings[1], key[2][0])
        ref = gathered.at[blk, :, base:base + width]
        i = index[key]
        pltpu.make_async_remote_copy(ref, ref, sems[0].at[i], sems[1].at[i], to, MESH).wait_recv()

    def onward(plan, o1):
        for side in ("f", "n"):
            if plan[0][1].reach[side]:
                gather_copy(plan, ("2", o1, (side, 1))).start()

    def gather_step(steps, meanwhile=lambda count: None):
        for plan in gathers:
            first, second = plan[0]
            for o1 in [None] + first.away:
                for o2 in [None] + second.away:
                    if dist(o1) + dist(o2) != steps:
                        continue
                    if o2 is None:
                        side, t = o1
                        gather_wait(plan, ("1", o1))
                        if t < first.reach[side]:
                            gather_copy(plan, ("1", (side, t + 1))).start()
                        onward(plan, o1)
                    else:
                        side, t = o2
                        gather_wait(plan, ("2", o1, o2))
                        if t < second.reach[side]:
                            gather_copy(plan, ("2", o1, (side, t + 1))).start()
                    meanwhile(3)

    def begin(plan):
        for side in ("f", "n"):
            if plan[0][0].reach[side]:
                gather_copy(plan, ("1", (side, 1))).start()
        onward(plan, None)

    grad_weight = jnp.zeros((cap, 1), F32)
    for which, at, width in ((0, 0, rs_a), (1, rs_a, rs_b)):
        total = reduced(plans[which])
        gate, up, bk = (total[:, j * width:(j + 1) * width] for j in range(3))
        sig = jax.nn.sigmoid(gate)
        active = gate * sig
        product = active * up
        grad_weight = grad_weight + jnp.sum(bk * product, axis=1, keepdims=True)
        scaled = weight_col * bk
        results = (
            (weight_col * product).astype(BF16),
            (scaled * up * sig * (1.0 + gate * (1.0 - sig))).astype(BF16),
            (scaled * active).astype(BF16),
        )
        for j, value in enumerate(results):
            for lo, hi, start, n in ((0, ag_a, 0, ag_a), (ag_a, ag_a + ag_b, full_a, ag_b)):
                a, b = max(lo, at), min(hi, at + width)
                if a < b:
                    col = start + j * n + a - lo
                    gathered[mine, :, col:col + b - a] = value[:, a - at:b - at]
        for part, n in ((0, ag_a), (1, ag_a + ag_b)):
            if at < n <= at + width:
                begin(gathers[part])

    rounded = grad_weight.astype(BF16).astype(F32)
    dp_send[...] = jnp.sum(jnp.where(diagonal, rounded, 0.0), axis=0, keepdims=True)

    def dp_copy(slot, where):
        return pltpu.make_async_remote_copy(
            dp_send, dp_recv.at[slot], dp_s, dp_r.at[slot], {"expert": where}, MESH)

    @pl.when(jnp.logical_not(on_diagonal))
    def _():
        dp_copy(me, mine).start()

    for r in range(1, experts):
        dispatch_copy(r).wait_send()
    def source(o):
        return rx.origin(o[0]) * ring_y + ry.origin(o[1])

    homeward = sorted(offsets, key=lambda o: -dist(o[0]) - dist(o[1]))
    late = 8 if group >= 16 else group // 2
    for first in range(0, group, late):
        block = jnp.concatenate([rows[source(o)] for o in homeward[first:first + late]], axis=0).astype(F32)
        lanes = slice(first * cap, (first + late) * cap)
        x_t[:, lanes] = block[:, 0:features].T.astype(BF16)
        dy_t[:, lanes] = block[:, features:2 * features].T.astype(BF16)

    def weight_chunk(part, c, m, j, first, last):
        at, n = ((0, ag_a), (ag_a, ag_b))[part]
        start = (0, full_a)[part] + c + j * n
        left, out = ((dy_t, g_down), (x_t, g_gate), (x_t, g_up))[j]
        right = jnp.concatenate([gathered[source(o), :, start:start + m] for o in homeward[first:last]], axis=0)
        value = nn(left[:, first * cap:last * cap], right)
        ref = out.at[at + c:at + c + m, :] if j == 0 else out.at[:, at + c:at + c + m]
        value = value.T if j == 0 else value
        ref[...] = value if first else ref[...] + value

    chunks = [
        (part, c, m, j) for part, n in enumerate((ag_a, ag_b)) for c, m in pieces(n) for j in range(3)]
    todo = list(chunks)

    def meanwhile(count):
        for _ in range(min(count, len(todo))):
            weight_chunk(*todo.pop(0), late, group)

    gather_step(1)
    gather_step(2)

    def spread_copy(r):
        return pltpu.make_async_remote_copy(
            spread, spread, bc_s.at[r], bc_r, {"dp": lax.rem(me + r, group)}, MESH)

    @pl.when(on_diagonal)
    def _():
        for r in range(1, experts):
            prob_copy(r).wait_send()
            dp_copy(lax.rem(me + r, experts), lax.rem(me + r, experts)).wait_recv()
        dp_recv[me] = dp_send[...]
        values = dp_recv[...].reshape(experts, 128).astype(BF16)
        lane = iota((tok, 128), 1)
        ids_col = nt(eye_t, ids_t.astype(BF16))
        result = jnp.zeros((tok, 128), F32)
        for k in range(top):
            pick = jnp.where(ids_col[:, k:k + 1] == iota((tok, experts), 1).astype(F32), 1.0, 0.0)
            row = nn(pick.astype(BF16), values)
            place = jnp.sum(jnp.where(pick > 0.5, rank_t, 0.0), axis=1, keepdims=True)
            found = jnp.sum(jnp.where(lane.astype(F32) == place, row, 0.0), axis=1, keepdims=True)
            result = jnp.where(lane == k, found, result)
        eye = jnp.where(iota((16, 128), 0) == iota((16, 128), 1), 1.0, 0.0).astype(BF16)
        spread[...] = jnp.zeros_like(spread)
        spread[:, 0:tok] = nt(eye, result.astype(BF16)).astype(BF16)
        for r in range(1, group):
            spread_copy(r).start()

    def return_copy(i, to):
        return pltpu.make_async_remote_copy(
            dx_send.at[i], back.at[me], ret_s.at[i], ret_r.at[me], {"expert": to}, MESH)

    def send_home(low, high):
        wave = [o for o in homeward if low <= dist(o[0]) + dist(o[1]) <= high]
        lo, count = homeward.index(wave[0]), len(wave)
        total = jnp.zeros((count * cap, features), F32)
        for part, (at, n) in enumerate(((0, ag_a), (ag_a, ag_b))):
            for j, w in ((1, w_gate), (2, w_up)):
                begin_at = (0, full_a)[part] + j * n
                left = jnp.concatenate([gathered[source(o), :, begin_at:begin_at + n] for o in wave], axis=0)
                total = total + nt(left, w[:, at:at + n])
        dx_send[lo:lo + count] = total.astype(BF16).reshape(count, cap, features)
        for i in range(lo, lo + count):
            to = source(homeward[i])

            @pl.when(to != me)
            def _():
                return_copy(i, to).start()

            @pl.when(to == me)
            def _():
                back[me] = dx_send[i]

    bounds = SENDS
    sent = -1
    for steps in range(3, furthest + 1):
        gather_step(steps, meanwhile if steps >= furthest - 1 else lambda count: None)
        if steps in bounds or steps == furthest:
            send_home(sent + 1, steps)
            sent = steps

    meanwhile(len(todo))
    for chunk in chunks:
        weight_chunk(*chunk, 0, late)
    stores = [
        pltpu.make_async_copy(src, dst, store_s.at[i])
        for i, (src, dst) in enumerate(((g_gate, o_gate), (g_up, o_up), (g_down, o_down)))
    ]
    for copy in stores:
        copy.start()

    @pl.when(jnp.logical_not(on_diagonal))
    def _():
        spread_copy(1).wait_recv()
        dp_copy(me, mine).wait_send()

    @pl.when(on_diagonal)
    def _():
        for r in range(1, group):
            spread_copy(r).wait_send()

    o_probs[...] = spread[0:top, 0:tok]
    for plan in plans:
        for key in plan[4]:
            one_copy(plan, key).wait_send()
        for key in plan[5]:
            two_copy(plan, key).wait_send()
    for plan in gathers:
        for key in plan[4]:
            gather_copy(plan, key).wait_send()
    for r in range(1, experts):
        sender = lax.rem(me + r, experts)
        pltpu.make_async_remote_copy(
            dx_send.at[0], back.at[sender], ret_s.at[0], ret_r.at[sender], {"expert": sender}, MESH).wait_recv()
    o_tokens[...] = nn(hot_t[...], back[...].reshape(slots, features)).astype(BF16)
    for i, o in enumerate(homeward):
        to = source(o)

        @pl.when(to != me)
        def _():
            return_copy(i, to).wait_send()
    for copy in stores:
        copy.wait()


def carry(parts, *refs):
    ins, outs, held, in_s, out_s = refs[:5], refs[5:10], refs[10:15], refs[15], refs[16]
    reads, writes = [], []
    for src, dst, mid in zip(ins, outs, held):
        rows = src.shape[0]
        cuts = parts if rows > 32 else 1
        for c in range(cuts):
            at, i = slice(c * rows // cuts, (c + 1) * rows // cuts), len(reads)
            reads.append(pltpu.make_async_copy(src.at[at], mid.at[at], in_s.at[i]))
            writes.append(pltpu.make_async_copy(mid.at[at], dst.at[at], out_s.at[i]))
    for copy in reads:
        copy.start()
    for read, write in zip(reads, writes):
        read.wait()
        write.start()
    for copy in writes:
        copy.wait()


def per_device(tokens, grad_out, expert_ids, probs, gate_weight, up_weight, down_weight):
    tok, features = tokens.shape
    top = expert_ids.shape[1]
    hidden = gate_weight.shape[2]
    experts, group = lax.axis_size("expert"), lax.axis_size("dp")
    cap = min(tok, 2 * tok * top // experts)
    ring_x, ring_y = RING_X, group // RING_X
    slots = experts * cap
    wide_a, wide_b = 3 * RS_SPLIT[0], 3 * RS_SPLIT[1]
    n_a1, n_a2 = (ring_x - 1) * ring_y, ring_y - 1
    n_b1, n_b2 = (ring_y - 1) * ring_x, ring_x - 1
    vmem = pltpu.VMEM
    dma = pltpu.SemaphoreType.DMA
    buffers = [
        vmem((features, hidden), BF16), vmem((features, hidden), BF16), vmem((hidden, features), BF16),
        vmem((features, hidden), F32), vmem((features, hidden), F32), vmem((hidden, features), F32),
        vmem((slots, tok), BF16), vmem((tok, slots), BF16),
        vmem((experts, cap, 2 * features), BF16), vmem((experts, cap, 2 * features), BF16),
        vmem((features, slots), BF16), vmem((features, slots), BF16),
        vmem((experts, 1, 128), F32), vmem((1, 128), F32),
        vmem((group, cap, 3 * hidden), F32),
        vmem((n_a1, cap, wide_a), BF16), vmem((n_a1, cap, wide_a), BF16),
        vmem((n_a2, cap, wide_a), F32), vmem((n_a2, cap, wide_a), F32),
        vmem((n_a2, cap, wide_a), BF16), vmem((n_a2, cap, wide_a), BF16),
        vmem((n_b1, cap, wide_b), BF16), vmem((n_b1, cap, wide_b), BF16),
        vmem((n_b2, cap, wide_b), F32), vmem((n_b2, cap, wide_b), F32),
        vmem((group, cap, 3 * hidden), BF16),
        vmem((experts, cap, features), BF16), vmem((experts, cap, features), BF16),
        vmem((1, 128), F32), vmem((experts, 1, 128), F32), vmem((16, 128), BF16),
    ]
    sems = [
        dma((3,)), dma((3,)),
        dma((experts,)), dma((experts,)), dma((experts,)), dma(()),
        dma((n_a1,)), dma((n_a1,)), dma((n_a2,)), dma((n_a2,)),
        dma((n_b1,)), dma((n_b1,)), dma((n_b2,)), dma((n_b2,)),
        dma((n_b2 * ring_y + n_a2,)), dma((n_b2 * ring_y + n_a2,)),
        dma((n_a2 * ring_x + n_b2,)), dma((n_a2 * ring_x + n_b2,)),
        dma((experts,)), dma((experts,)), dma(()), dma((experts,)), dma((group,)), dma(()),
    ]
    flops = 2 * slots * features * hidden * 8
    out = pl.pallas_call(
        functools.partial(kernel, ring_x, ring_y, cap, RS_SPLIT, AG_SPLIT),
        out_shape=(
            jax.ShapeDtypeStruct((tok, features), BF16),
            jax.ShapeDtypeStruct((top, tok), BF16),
            jax.ShapeDtypeStruct((features, hidden), F32),
            jax.ShapeDtypeStruct((features, hidden), F32),
            jax.ShapeDtypeStruct((hidden, features), F32),
        ),
        in_specs=[pl.BlockSpec(memory_space=pltpu.VMEM)] * 4 + [pl.BlockSpec(memory_space=pl.ANY)] * 3,
        out_specs=[pl.BlockSpec(memory_space=pltpu.VMEM)] * 2 + [pl.BlockSpec(memory_space=pl.ANY)] * 3,
        scratch_shapes=buffers + sems,
        compiler_params=pltpu.CompilerParams(
            collective_id=0, has_side_effects=True, vmem_limit_bytes=58 * 1024 * 1024),
        cost_estimate=pl.CostEstimate(flops=flops, bytes_accessed=4 * 1024 * 1024, transcendentals=0),
    )(tokens, grad_out, expert_ids.T, probs.T, gate_weight[0], up_weight[0], down_weight[0])
    out = pl.pallas_call(
        functools.partial(carry, CUTS),
        out_shape=[jax.ShapeDtypeStruct(o.shape, o.dtype) for o in out],
        in_specs=[pl.BlockSpec(memory_space=pl.ANY)] * 5,
        out_specs=[pl.BlockSpec(memory_space=pl.ANY)] * 5,
        scratch_shapes=[vmem(o.shape, o.dtype) for o in out] + [dma((2 + 3 * CUTS,))] * 2,
        compiler_params=pltpu.CompilerParams(vmem_limit_bytes=58 * 1024 * 1024),
        cost_estimate=pl.CostEstimate(flops=0, bytes_accessed=5 * 1024 * 1024, transcendentals=0),
    )(*out)
    grad_tokens, grad_probs, grad_gate, grad_up, grad_down = out
    return grad_tokens, grad_probs.T, grad_gate[None], grad_up[None], grad_down[None]


def solution(mesh):
    return jax.shard_map(
        per_device,
        mesh=mesh,
        in_specs=(
            P("expert", "dp"),
            P("expert", "dp"),
            P("expert", None),
            P("expert", None),
            P("expert", "dp", None),
            P("expert", "dp", None),
            P("expert", None, "dp"),
        ),
        out_specs=(
            P("expert", "dp"),
            P("expert", None),
            P("expert", "dp", None),
            P("expert", "dp", None),
            P("expert", None, "dp"),
        ),
        check_vma=False,
    )
```
